1024 devices in a mesh: row: 16 (over y, z_hi), col: 8 (over z_lo, core), feat: 8 (over x).
Axes of the slice: x: 8, y: 8, z: 8 (z_hi: 2, z_lo: 4; z = z_hi * 4 + z_lo), core: 2. Of those that a mesh axis runs over, the one named last changes fastest.
Arguments:
- features: bfloat16 [131072, 256], P(('col', 'row'), 'feat'), may hold values from -6 to 6
- weight: bfloat16 [256, 256], P('feat'), may hold values from -0.375 to 0.375
- grad_out: bfloat16 [131072, 256], P(('row', 'col', 'feat')), may hold values from -6 to 6
- adjacency: bfloat16 [24576, 128, 128], P(('row', 'col')), may hold values from 0 to 0.029907227
- tile_rows: int32 [24576], P(('row', 'col')), may hold values from 0 to 63, as said below
- tile_cols: int32 [24576], P(('row', 'col')), may hold values from 0 to 127
- tile_count: int32 [128], P(('row', 'col')), may hold values from 48 to 192, as said below
Outputs:
- activated: bfloat16 [131072, 256], P(('row', 'col', 'feat'))
- weight_grad: float32 [256, 256], P('feat')
- feature_grad: float32 [131072, 256], P(('col', 'row'), 'feat')
The draws below stay inside these ranges and needn't reach their ends.
Inputs may be any that keep to these rules, and one draw needn't show every extreme that they name: Within one device pair the positions (tile_rows, tile_cols) of its 192 slots are all different. `tile_count`: some device pair has all 192 slots live.
All inputs are finite; a program needn't handle non-finite values.
Results may differ from the reference program's by a relative error of at most 0.0049.
Values may be sent and summed in bfloat16 or wider, within the bound.
No kernel may reach another device: no remote copies, remote signals or barrier semaphores. Data moves between devices by JAX's collectives and lax.ppermute only.
A program may use at most 32 MiB of HBM per device.

```python
import jax
import jax.numpy as jnp
from jax import lax

F = 256
TB = 128
TCAP = 192
BR_DEV = 64
N_NODES = 131072
BC_DEV = 128
PAIRS = 128
TILES = 24576
N_COL = 8


def tile_positions(key):
    key_list = jax.random.split(key, PAIRS)

    def pick_slots(slot_key):
        return jax.random.permutation(slot_key, BR_DEV * BC_DEV)[:TCAP]
    return jax.vmap(pick_slots)(key_list).reshape(-1).astype(jnp.int32)


def draw_tile_rows(key, part):
    positions = tile_positions(key)
    return (positions // BC_DEV).astype(jnp.int32)


def draw_tile_cols(key, part):
    positions = tile_positions(key)
    return (positions % BC_DEV).astype(jnp.int32)


def draw_tile_count(key, part):
    key = jax.random.fold_in(key, 3)
    first_key, second_key, third_key, fourth_key = jax.random.split(key, 4)
    quiet_count = jax.random.randint(first_key, (PAIRS,), TCAP // 4, TCAP // 2 + 1)
    busy_count = jax.random.randint(second_key, (PAIRS,), TCAP // 2, TCAP + 1)
    chooser = jax.random.randint(third_key, (PAIRS,), 0, 8)
    count_list = jnp.where(chooser == 0, busy_count, quiet_count)
    full_device = jax.random.randint(fourth_key, (), 0, PAIRS)
    count_list = jnp.where(jnp.arange(PAIRS) == full_device, TCAP, count_list)
    return count_list.astype(jnp.int32)


def block_levels(stream_key, dims, cuts, least, high):
    def one(axis_at, shards_of):
        draws = jax.random.uniform(jax.random.fold_in(jax.random.fold_in(stream_key, 6), axis_at), (shards_of,), jnp.float32, least / len(cuts), high / len(cuts))
        return jnp.repeat(jnp.exp(draws), dims[axis_at] // shards_of).reshape((-1,) + (1,) * (len(dims) - axis_at - 1))

    level = one(*cuts[0])
    for cut in cuts[1:]:
        level = level * one(*cut)
    return level


def scatter_about(stream_key, dims, width, most, cuts=(), kind=jnp.bfloat16):
    drawn = width * jax.random.normal(stream_key, dims, jnp.float32)
    if cuts:
        drawn = drawn * block_levels(stream_key, dims, cuts, -0.22, 0.18)
    return jnp.clip(drawn, -most, most).astype(kind)


def setup_inputs(seed: int = 0) -> dict:
    keys = jax.random.split(jax.random.key(seed), 8)
    features = scatter_about(keys[0], (N_NODES, F), 1.0, 6.0, ((0, 128), (1, 8)))
    weight = scatter_about(keys[1], (F, F), F ** -0.5, 0.375, ((0, 8),))
    grad_out = scatter_about(keys[2], (N_NODES, F), 1.0, 6.0, ((0, 1024),))
    adjacency = jnp.clip(0.029907227 * jax.random.uniform(keys[3], (TILES, TB, TB), jnp.float32) ** block_levels(keys[3], (TILES, TB, TB), ((0, 128),), -0.2, 0.2), 0.0, 0.029907227).astype(jnp.bfloat16)
    tile_rows = draw_tile_rows(jax.random.fold_in(keys[7], 71), 0)
    tile_cols = draw_tile_cols(jax.random.fold_in(keys[7], 71), 0)
    tile_count = draw_tile_count(jax.random.fold_in(keys[7], 71), 0)
    return {"features": features, "weight": weight, "grad_out": grad_out, "adjacency": adjacency, "tile_rows": tile_rows, "tile_cols": tile_cols, "tile_count": tile_count}


def reference(features, weight, grad_out, adjacency, tile_rows, tile_cols, tile_count):
    feature_total_count = features.shape[1]
    tile_extent = adjacency.shape[1]
    row_span = BR_DEV * tile_extent
    column_extent = BC_DEV * tile_extent
    highest_precision = lax.Precision.HIGHEST
    adj_groups = adjacency.reshape(PAIRS, TCAP, tile_extent, tile_extent)
    row_lists = tile_rows.reshape(PAIRS, TCAP)
    col_lists = tile_cols.reshape(PAIRS, TCAP)
    devices = jnp.arange(PAIRS, dtype=jnp.int32)
    slot_index = jnp.arange(TCAP, dtype=jnp.int32)
    row_identifiers = jnp.arange(BR_DEV, dtype=jnp.int32)
    col_ids = jnp.arange(BC_DEV, dtype=jnp.int32)

    def forward_step(running, inputs):
        adj_tiles, slot_rows, slot_cols, live_count, device = inputs
        live_mask = (slot_index < live_count).astype(jnp.float32)
        source = lax.dynamic_slice_in_dim(features, (device % N_COL) * column_extent, column_extent, 0)
        chosen = source.reshape(BC_DEV, tile_extent, feature_total_count)[slot_cols].astype(jnp.float32)
        products = jnp.einsum("tab,tbf->taf", adj_tiles.astype(jnp.float32), chosen, precision=highest_precision)
        one_hot = (slot_rows[None, :] == row_identifiers[:, None]).astype(jnp.float32) * live_mask[None, :]
        block_sum = jnp.einsum("rt,taf->raf", one_hot, products, precision=highest_precision).reshape(row_span, feature_total_count)
        row_start = (device // N_COL) * row_span
        current = lax.dynamic_slice_in_dim(running, row_start, row_span, 0)
        return lax.dynamic_update_slice_in_dim(running, current + block_sum, row_start, 0), None

    summed, unused = lax.scan(forward_step, jnp.zeros(features.shape, jnp.float32),
                              (adj_groups, row_lists, col_lists, tile_count, devices))
    pre_act = jnp.dot(summed, weight.astype(jnp.float32), precision=highest_precision)
    gate_value = jax.nn.sigmoid(pre_act)
    activated = (pre_act * gate_value).astype(jnp.bfloat16)
    derivative = gate_value * (1.0 + pre_act * (1.0 - gate_value))
    grad_pre = (grad_out.astype(jnp.float32) * derivative).astype(jnp.bfloat16)
    weight_grad = jnp.dot(summed.T, grad_pre.astype(jnp.float32), precision=highest_precision)
    weight_grad = weight_grad * (1.0 / (features.shape[0] ** 0.5))
    projected = jnp.dot(grad_pre, weight.T, preferred_element_type=jnp.float32).astype(jnp.bfloat16)

    def backward_step(running, inputs):
        adj_tiles, slot_rows, slot_cols, live_count, device = inputs
        live_mask = (slot_index < live_count).astype(jnp.float32)
        source = lax.dynamic_slice_in_dim(projected, (device // N_COL) * row_span, row_span, 0)
        chosen = source.reshape(BR_DEV, tile_extent, feature_total_count)[slot_rows].astype(jnp.float32)
        backward_pieces = jnp.einsum("tab,taf->tbf", adj_tiles.astype(jnp.float32), chosen, precision=highest_precision)
        column_onehot = (slot_cols[None, :] == col_ids[:, None]).astype(jnp.float32) * live_mask[None, :]
        spread_factor = jnp.einsum("oi,ihn->ohn", column_onehot, backward_pieces, precision=highest_precision).reshape(column_extent, feature_total_count)
        col_start = (device % N_COL) * column_extent
        current = lax.dynamic_slice_in_dim(running, col_start, column_extent, 0)
        return lax.dynamic_update_slice_in_dim(running, current + spread_factor, col_start, 0), None

    feature_grad, unused = lax.scan(backward_step, jnp.zeros(features.shape, jnp.float32),
                                    (adj_groups, row_lists, col_lists, tile_count, devices))
    return activated, weight_grad, feature_grad
```

```python
import functools
import math

import jax
import jax.numpy as jnp
from jax import lax
from jax.experimental import pallas as pl
from jax.experimental.pallas import tpu as pltpu
from jax.sharding import PartitionSpec as P

BR_DEV = 64
CHUNK = 32
UNROLL = 8
VMEM_LIMIT = 40 * 1024 * 1024
NT = (((1,), (1,)), ((), ()))
NN = (((1,), (0,)), ((), ()))
TN = (((0,), (0,)), ((), ()))


def dot(a, b, dims):
    return lax.dot_general(a, b, dims, preferred_element_type=jnp.float32)


def accumulate_tiles(count, source, adj_ref, acc_ref, target_of, dims):
    first = pl.program_id(0) * CHUNK

    @pl.when(first < count)
    def _():
        @pl.loop(0, CHUNK // UNROLL)
        def _(group):
            base = group * UNROLL
            terms = []
            for u in range(UNROLL):
                slot = first + base + u
                term = dot(source(slot), adj_ref[base + u], dims)
                terms.append(jnp.where(slot < count, term, 0.0))
            for u in range(UNROLL):
                target = target_of(first + base + u)
                acc_ref[target] += terms[u]


def forward_kernel(rows, cols, count, adj_ref, feat_ref, out_ref, acc_ref):
    @pl.when(pl.program_id(0) == 0)
    def _():
        acc_ref[...] = jnp.zeros_like(acc_ref)

    accumulate_tiles(
        count[0], lambda s: feat_ref[cols[s]], adj_ref, acc_ref, lambda s: rows[s], NT
    )

    @pl.when(pl.program_id(0) == pl.num_programs(0) - 1)
    def _():
        out_ref[...] = acc_ref[...].astype(out_ref.dtype)


def dense_kernel(feat_index, summed_ref, wide_ref, weight_ref, out_ref, act_ref):
    feats, blocks, width, extent = summed_ref.shape
    own = feat_index[0]
    weight_all = wide_ref[:, :width].reshape(feats * width, feats * width)
    weight_own = weight_ref[...]
    weight_term = jnp.zeros((width, feats * width), jnp.float32)
    for block in range(blocks):
        summed = summed_ref[:, block].reshape(feats * width, extent)
        pre_act = dot(summed, weight_all, TN)
        gate = jax.nn.sigmoid(pre_act)
        grad_out = wide_ref[block, width:].astype(jnp.float32)
        derivative = gate * (1.0 + pre_act * (1.0 - gate))
        grad_pre = (grad_out * derivative).astype(jnp.bfloat16)
        out_ref[block] = dot(weight_own, grad_pre, NT).astype(out_ref.dtype)
        weight_term += dot(summed_ref[own, block], grad_pre, NN)

        @pl.when(own == block)
        def _():
            act_ref[...] = (pre_act * gate).astype(act_ref.dtype)

    for part in range(feats * width // extent):
        out_ref[blocks + part] = weight_term[:, part * extent : (part + 1) * extent].astype(
            out_ref.dtype
        )


def backward_kernel(rows, cols, count, adj_ref, proj_ref, out_ref, acc_ref):
    per_col = BR_DEV // proj_ref.shape[0]
    row_devices, blocks = out_ref.shape[0], acc_ref.shape[0] // out_ref.shape[0]

    @pl.when(pl.program_id(0) == 0)
    def _():
        acc_ref[...] = jnp.zeros_like(acc_ref)

    accumulate_tiles(
        count[0],
        lambda s: proj_ref[rows[s] // per_col, rows[s] % per_col],
        adj_ref,
        acc_ref,
        lambda s: cols[s],
        NN,
    )

    @pl.when(pl.program_id(0) == pl.num_programs(0) - 1)
    def _():
        terms = jnp.sum(proj_ref[:, per_col:].astype(jnp.float32), axis=0).astype(out_ref.dtype)
        for row in range(row_devices):
            out_ref[row, :blocks] = acc_ref[row * blocks : (row + 1) * blocks].astype(
                out_ref.dtype
            )
            out_ref[row, blocks:] = terms


def tile_call(kernel, scalars, adjacency, source, out_shape, acc_shape):
    slots, extent, _ = adjacency.shape
    whole = lambda shape: pl.BlockSpec(shape, lambda i, *_: (0,) * len(shape))
    return pl.pallas_call(
        kernel,
        out_shape=jax.ShapeDtypeStruct(out_shape, jnp.bfloat16),
        grid_spec=pltpu.PrefetchScalarGridSpec(
            num_scalar_prefetch=3,
            grid=(slots // CHUNK,),
            in_specs=[
                pl.BlockSpec((CHUNK, extent, extent), lambda i, *_: (i, 0, 0)),
                whole(source.shape),
            ],
            out_specs=whole(out_shape),
            scratch_shapes=[pltpu.VMEM(acc_shape, jnp.float32)],
        ),
        compiler_params=pltpu.CompilerParams(vmem_limit_bytes=VMEM_LIMIT),
    )(*scalars, adjacency, source)


def local(features, weight, grad_out, adjacency, tile_rows, tile_cols, tile_count):
    nodes, width = features.shape
    extent = adjacency.shape[1]
    rows, cols, feats = (lax.axis_size(name) for name in ("row", "col", "feat"))
    full = feats * width
    blocks = nodes // extent
    scalars = (tile_rows, tile_cols, tile_count)

    wide = lax.all_gather(
        jnp.concatenate([weight, grad_out], axis=0), "feat", axis=0, tiled=True
    ).reshape(feats, width + extent, full)

    own = features.T.reshape(width, blocks, extent).transpose(1, 0, 2)
    gathered = lax.all_to_all(
        jnp.broadcast_to(own[None], (rows,) + own.shape), "row", 0, 0, tiled=False
    )
    gathered = gathered.reshape(rows * blocks, width, extent)

    partial_value = tile_call(
        forward_kernel,
        scalars,
        adjacency,
        gathered,
        (BR_DEV, width, extent),
        (BR_DEV, width, extent),
    )
    per_col = BR_DEV // cols
    terms = lax.all_to_all(
        partial_value.reshape(cols, per_col, width, extent), "col", 0, 0, tiled=False
    )
    summed = jnp.sum(terms.astype(jnp.float32), axis=0).astype(jnp.bfloat16)
    summed = lax.all_gather(summed, "feat", axis=0, tiled=False)

    parts = full // extent
    feat_index = lax.axis_index("feat").astype(jnp.int32).reshape(1)
    vmem = pl.BlockSpec(memory_space=pltpu.VMEM)
    outgoing, activated = pl.pallas_call(
        dense_kernel,
        out_shape=(
            jax.ShapeDtypeStruct((per_col + parts, width, extent), jnp.bfloat16),
            jax.ShapeDtypeStruct((extent, full), jnp.bfloat16),
        ),
        in_specs=[pl.BlockSpec(memory_space=pltpu.SMEM), vmem, vmem, vmem],
        out_specs=(vmem, vmem),
        compiler_params=pltpu.CompilerParams(vmem_limit_bytes=VMEM_LIMIT),
    )(feat_index, summed, wide, weight)

    projected = lax.all_gather(outgoing, "col", axis=0, tiled=False)
    pieces = tile_call(
        backward_kernel,
        scalars,
        adjacency,
        projected,
        (rows, blocks + parts, width, extent),
        (rows * blocks, width, extent),
    )
    pieces = lax.all_to_all(pieces, "row", 0, 0, tiled=False)
    total = jnp.sum(pieces.astype(jnp.float32), axis=0)
    total = total.transpose(1, 0, 2).reshape(width, (blocks + parts) * extent)
    feature_grad = total[:, :nodes].T
    weight_grad = total[:, nodes:] * (1.0 / math.sqrt(nodes * rows * cols))
    return (activated, weight_grad, feature_grad)


def solution(mesh):
    placed = (
        P(("col", "row"), "feat"),
        P("feat", None),
        P(("row", "col", "feat"), None),
        P(("row", "col"), None, None),
        P(("row", "col")),
        P(("row", "col")),
        P(("row", "col")),
    )
    return jax.shard_map(
        local,
        mesh=mesh,
        in_specs=placed,
        out_specs=(P(("row", "col", "feat"), None), P("feat", None), P(("col", "row"), "feat")),
        check_vma=False,
    )
```

```python
import math

import jax
import jax.numpy as jnp
from jax import lax
from jax.experimental import pallas as pl
from jax.experimental.pallas import tpu as pltpu
from jax.sharding import PartitionSpec as P

CHUNK = 24
UNROLL = 8
PIECE = 8
VMEM_LIMIT = 58 * 1024 * 1024
NT = (((1,), (1,)), ((), ()))
NN = (((1,), (0,)), ((), ()))
TN = (((0,), (0,)), ((), ()))


def dot(a, b, dims):
    return lax.dot_general(a, b, dims, preferred_element_type=jnp.float32)


def accumulate_tiles(count, source, adj_ref, acc_ref, target_of, dims):
    first = pl.program_id(0) * CHUNK

    @pl.when(first < count)
    def _():
        @pl.loop(0, CHUNK // UNROLL)
        def _(group):
            base = group * UNROLL
            terms = []
            for u in range(UNROLL):
                slot = first + base + u
                term = dot(source(slot), adj_ref[base + u], dims)
                terms.append(jnp.where(slot < count, term, 0.0))
            for u in range(UNROLL):
                target = target_of(first + base + u)
                acc_ref[target] += terms[u]


def forward_kernel(rows, cols, count, adj_ref, feat_ref, out_ref, acc_ref):
    extent = adj_ref.shape[1]
    blocks = feat_ref.shape[2] // extent

    @pl.when(pl.program_id(0) == 0)
    def _():
        acc_ref[...] = jnp.zeros_like(acc_ref)

    def source(slot):
        col = cols[slot]
        start = pl.multiple_of((col % blocks) * extent, extent)
        return feat_ref[col // blocks, :, pl.ds(start, extent)]

    accumulate_tiles(count[0], source, adj_ref, acc_ref, lambda s: rows[s], NT)

    @pl.when(pl.program_id(0) == pl.num_programs(0) - 1)
    def _():
        out_ref[...] = acc_ref[...].astype(out_ref.dtype)


def dense_kernel(terms_ref, weight_ref, grad_ref, out_ref, act_ref):
    cols, feats, width, extent = terms_ref.shape
    full = feats * width
    weight = weight_ref[...]
    summed = jnp.sum(terms_ref[...].astype(jnp.float32), axis=0).reshape(full, extent)
    high = summed.astype(jnp.bfloat16)
    low = (summed - high.astype(jnp.float32)).astype(jnp.bfloat16)
    pre_act = dot(high, weight, TN) + dot(low, weight, TN)
    gate = jax.nn.sigmoid(pre_act)
    act_ref[...] = (pre_act * gate).astype(act_ref.dtype)
    derivative = gate * (1.0 + pre_act * (1.0 - gate))
    grad_pre = (grad_ref[...].astype(jnp.float32) * derivative).astype(jnp.bfloat16)
    projected = dot(weight, grad_pre, NT).astype(out_ref.dtype)
    weight_term = dot(high, grad_pre, NN) + dot(low, grad_pre, NN)
    halves = full // extent
    for col in range(cols):
        for feat in range(feats):
            top = feat * width + (col // halves) * PIECE
            left = (col % halves) * extent
            out_ref[col * feats + feat, :width] = projected[feat * width : (feat + 1) * width]
            out_ref[col * feats + feat, width:] = weight_term[
                top : top + PIECE, left : left + extent
            ].astype(out_ref.dtype)


def backward_kernel(rows, cols, count, adj_ref, proj_ref, out_ref, acc_ref):
    row_devices = out_ref.shape[0]
    blocks, width = acc_ref.shape[0] // row_devices, acc_ref.shape[1]

    @pl.when(pl.program_id(0) == 0)
    def _():
        acc_ref[...] = jnp.zeros_like(acc_ref)

    accumulate_tiles(
        count[0], lambda s: proj_ref[rows[s], :width], adj_ref, acc_ref, lambda s: cols[s], NN
    )

    @pl.when(pl.program_id(0) == pl.num_programs(0) - 1)
    def _():
        weight_term = jnp.sum(proj_ref[:, width:].astype(jnp.float32), axis=0)
        for row in range(row_devices):
            for block in range(blocks):
                out_ref[row, block * width : (block + 1) * width] = acc_ref[
                    row * blocks + block
                ].astype(out_ref.dtype)
            out_ref[row, blocks * width :] = weight_term.astype(out_ref.dtype)


def final_kernel(scale, pieces_ref, grad_ref, weight_ref):
    width, nodes = grad_ref.shape
    extent = pieces_ref.shape[2]
    for block in range(nodes // extent):
        grad_ref[:, block * extent : (block + 1) * extent] = jnp.sum(
            pieces_ref[:, block * width : (block + 1) * width].astype(jnp.float32), axis=0
        )
    rest = pieces_ref[:, nodes // extent * width :].astype(jnp.float32)
    weight_ref[...] = jnp.sum(rest, axis=0) * scale


def tile_call(kernel, scalars, adjacency, source, out_shape, acc_shape):
    slots, extent, _ = adjacency.shape
    whole = lambda shape: pl.BlockSpec(shape, lambda i, *_: (0,) * len(shape))
    return pl.pallas_call(
        kernel,
        out_shape=jax.ShapeDtypeStruct(out_shape, jnp.bfloat16),
        grid_spec=pltpu.PrefetchScalarGridSpec(
            num_scalar_prefetch=3,
            grid=(slots // CHUNK,),
            in_specs=[
                pl.BlockSpec((CHUNK, extent, extent), lambda i, *_: (i, 0, 0)),
                whole(source.shape),
            ],
            out_specs=whole(out_shape),
            scratch_shapes=[pltpu.VMEM(acc_shape, jnp.float32)],
        ),
        compiler_params=pltpu.CompilerParams(vmem_limit_bytes=VMEM_LIMIT),
    )(*scalars, adjacency, source)


def local(features, weight, grad_out, adjacency, tile_rows, tile_cols, tile_count):
    nodes, width = features.shape
    extent = adjacency.shape[1]
    rows, cols, feats = (lax.axis_size(name) for name in ("row", "col", "feat"))
    full = feats * width
    blocks = nodes // extent
    owners = cols * feats
    scalars = (tile_rows, tile_cols, tile_count)
    vmem = pl.BlockSpec(memory_space=pltpu.VMEM)

    weight_all = lax.all_gather(weight, "feat", axis=0, tiled=True)
    own = features.T
    gathered = lax.all_to_all(
        jnp.broadcast_to(own[None], (rows,) + own.shape), "row", 0, 0, tiled=False
    )
    gathered, weight_all = lax.optimization_barrier((gathered, weight_all))

    terms = tile_call(
        forward_kernel,
        scalars,
        adjacency,
        gathered,
        (owners, width, extent),
        (owners, width, extent),
    )
    terms = lax.all_to_all(terms, ("col", "feat"), 0, 0, tiled=False)
    outgoing, activated = pl.pallas_call(
        dense_kernel,
        out_shape=(
            jax.ShapeDtypeStruct((owners, width + PIECE, extent), jnp.bfloat16),
            jax.ShapeDtypeStruct((extent, full), jnp.bfloat16),
        ),
        in_specs=[vmem, vmem, vmem],
        out_specs=(vmem, vmem),
    )(terms.reshape(cols, feats, width, extent), weight_all, grad_out)

    projected = lax.all_to_all(outgoing, ("col", "feat"), 0, 0, tiled=False)
    pieces = tile_call(
        backward_kernel,
        scalars,
        adjacency,
        projected,
        (rows, blocks * width + PIECE, extent),
        (rows * blocks, width, extent),
    )
    pieces = lax.all_to_all(pieces, "row", 0, 0, tiled=False)
    scale = 1.0 / math.sqrt(nodes * rows * cols)
    feature_grad, weight_piece = pl.pallas_call(
        lambda *refs: final_kernel(scale, *refs),
        out_shape=(
            jax.ShapeDtypeStruct((width, nodes), jnp.float32),
            jax.ShapeDtypeStruct((PIECE, extent), jnp.float32),
        ),
        in_specs=[vmem],
        out_specs=(vmem, vmem),
    )(pieces)
    weight_grad = lax.all_gather(weight_piece, "col", axis=0, tiled=True)
    weight_grad = weight_grad.reshape(width // PIECE, full // extent, PIECE, extent)
    weight_grad = weight_grad.transpose(0, 2, 1, 3).reshape(width, full)
    return (activated, weight_grad, feature_grad.T)


def solution(mesh):
    placed = (
        P(("col", "row"), "feat"),
        P("feat", None),
        P(("row", "col", "feat"), None),
        P(("row", "col"), None, None),
        P(("row", "col")),
        P(("row", "col")),
        P(("row", "col")),
    )
    return jax.shard_map(
        local,
        mesh=mesh,
        in_specs=placed,
        out_specs=(P(("row", "col", "feat"), None), P("feat", None), P(("col", "row"), "feat")),
        check_vma=False,
    )
```

```python
import math

import jax
import jax.numpy as jnp
from jax import lax
from jax.experimental import pallas as pl
from jax.experimental.pallas import tpu as pltpu
from jax.sharding import PartitionSpec as P

UNROLL = 8
PIECE = 16
CORES = 2
VMEM_LIMIT = 24 * 1024 * 1024
NT = (((1,), (1,)), ((), ()))
NN = (((1,), (0,)), ((), ()))
TN = (((0,), (0,)), ((), ()))


def dot(a, b, dims):
    return lax.dot_general(a, b, dims, preferred_element_type=jnp.float32)


def stage_kernel(source_ref, out_ref, done):
    copy = pltpu.make_async_copy(source_ref, out_ref, done)
    copy.start()
    copy.wait()


def accumulate_tiles(count, source, adj_ref, acc_ref, target_of, dims):
    acc_ref[...] = jnp.zeros_like(acc_ref)

    @pl.loop(0, adj_ref.shape[0] // UNROLL)
    def _(group):
        first = group * UNROLL

        @pl.when(first < count)
        def _():
            terms = []
            for u in range(UNROLL):
                term = dot(source(first + u), adj_ref[first + u], dims)
                terms.append(jnp.where(first + u < count, term, 0.0))
            for u in range(UNROLL):
                target = target_of(first + u)
                acc_ref[target] += terms[u]


def forward_kernel(core, rows, cols, count, adj_ref, feat_ref, keep_ref, send_ref, acc_ref):
    extent = adj_ref.shape[1]
    blocks = feat_ref.shape[2] // extent

    def source(slot):
        col = cols[slot]
        start = pl.multiple_of((col % blocks) * extent, extent)
        return feat_ref[col // blocks, :, pl.ds(start, extent)]

    accumulate_tiles(count[0], source, adj_ref, acc_ref, lambda s: rows[s], NT)
    near, feats = keep_ref.shape[:2]
    for pair in range(near):
        keep_ref[pair] = acc_ref[pl.ds((pair * CORES + core[0]) * feats, feats)]
        send_ref[pair] = acc_ref[pl.ds((pair * CORES + 1 - core[0]) * feats, feats)]


def dense_kernel(terms_ref, weight_ref, grad_ref, out_ref, act_ref):
    near, feats, width, extent = terms_ref.shape
    full = feats * width
    weight = weight_ref[...]
    summed = jnp.sum(terms_ref[...].astype(jnp.float32), axis=0).reshape(full, extent)
    high = summed.astype(jnp.bfloat16)
    low = (summed - high.astype(jnp.float32)).astype(jnp.bfloat16)
    pre_act = dot(high, weight, TN) + dot(low, weight, TN)
    gate = jax.nn.sigmoid(pre_act)
    act_ref[...] = (pre_act * gate).astype(act_ref.dtype)
    derivative = gate * (1.0 + pre_act * (1.0 - gate))
    grad_pre = (grad_ref[...].astype(jnp.float32) * derivative).astype(jnp.bfloat16)
    projected = dot(weight, grad_pre, NT).astype(out_ref.dtype)
    weight_term = (dot(high, grad_pre, NN) + dot(low, grad_pre, NN)).astype(out_ref.dtype)
    halves = full // extent
    for pair in range(near):
        for feat in range(feats):
            top = feat * width + (pair // halves) * PIECE
            left = (pair % halves) * extent
            out_ref[pair * feats + feat, :width] = projected[feat * width : (feat + 1) * width]
            out_ref[pair * feats + feat, width:] = weight_term[
                top : top + PIECE, left : left + extent
            ]


def backward_kernel(
    core, rows, cols, count, adj_ref, mine_ref, other_ref, out_ref, proj_ref, acc_ref
):
    row_devices = out_ref.shape[0]
    blocks, width = acc_ref.shape[0] // row_devices, acc_ref.shape[1]
    feats = proj_ref.shape[2]
    for pair in range(proj_ref.shape[0]):
        part = slice(pair * feats, (pair + 1) * feats)
        proj_ref[pair, core[0]] = mine_ref[part, :width]
        proj_ref[pair, 1 - core[0]] = other_ref[part, :width]

    def source(slot):
        row = rows[slot]
        return proj_ref[row // (CORES * feats), (row // feats) % CORES, row % feats]

    accumulate_tiles(count[0], source, adj_ref, acc_ref, lambda s: cols[s], NN)
    weight_term = jnp.sum(mine_ref[:, width:].astype(jnp.float32), axis=0) + jnp.sum(
        other_ref[:, width:].astype(jnp.float32), axis=0
    )
    for row in range(row_devices):
        for block in range(blocks):
            out_ref[row, block * width : (block + 1) * width] = acc_ref[
                row * blocks + block
            ].astype(out_ref.dtype)
        out_ref[row, blocks * width :] = weight_term.astype(out_ref.dtype)


def final_kernel(scale, pieces_ref, grad_ref, weight_ref):
    width, nodes = grad_ref.shape
    extent = pieces_ref.shape[2]
    for block in range(nodes // extent):
        grad_ref[:, block * extent : (block + 1) * extent] = jnp.sum(
            pieces_ref[:, block * width : (block + 1) * width].astype(jnp.float32), axis=0
        )
    rest = pieces_ref[:, nodes // extent * width :].astype(jnp.float32)
    weight_ref[...] = jnp.sum(rest, axis=0) * scale


SMEM_SPEC = pl.BlockSpec(memory_space=pltpu.SMEM)
VMEM_SPEC = pl.BlockSpec(memory_space=pltpu.VMEM)


def stage(array):
    return pl.pallas_call(
        stage_kernel,
        out_shape=pltpu.VMEM(array.shape, array.dtype),
        in_specs=[pl.BlockSpec(memory_space=pltpu.HBM)],
        out_specs=VMEM_SPEC,
        scratch_shapes=[pltpu.SemaphoreType.DMA],
        compiler_params=pltpu.CompilerParams(vmem_limit_bytes=VMEM_LIMIT),
        cost_estimate=pl.CostEstimate(
            flops=0, bytes_accessed=2 * array.size * 2, transcendentals=0
        ),
    )(pltpu.with_memory_space_constraint(array, pltpu.HBM))


def tile_call(kernel, scalars, adjacency, sources, out_shapes, scratch):
    return pl.pallas_call(
        kernel,
        out_shape=out_shapes,
        in_specs=[SMEM_SPEC] * len(scalars) + [VMEM_SPEC] * (1 + len(sources)),
        out_specs=jax.tree.map(lambda _: VMEM_SPEC, out_shapes),
        scratch_shapes=scratch,
        compiler_params=pltpu.CompilerParams(vmem_limit_bytes=VMEM_LIMIT),
    )(*scalars, pltpu.with_memory_space_constraint(adjacency, pltpu.VMEM), *sources)


def local(features, weight, grad_out, adjacency, tile_rows, tile_cols, tile_count):
    nodes, width = features.shape
    extent = adjacency.shape[1]
    rows, near, feats = (lax.axis_size(name) for name in ("row", "near", "feat"))
    full = feats * width
    blocks = nodes // extent
    owners = near * feats
    swap = [(i, CORES - 1 - i) for i in range(CORES)]
    core = lax.axis_index("core").astype(jnp.int32).reshape(1)
    scalars = (core, tile_rows, tile_cols, tile_count)

    weight_all = lax.all_gather(weight, "feat", axis=0, tiled=True)
    adjacency = stage(adjacency)
    own = features.T
    gathered = lax.all_to_all(
        jnp.broadcast_to(own[None], (rows,) + own.shape), "row", 0, 0, tiled=False
    )
    gathered, weight_all, adjacency = lax.optimization_barrier((gathered, weight_all, adjacency))

    half = jax.ShapeDtypeStruct((near, feats, width, extent), jnp.float32)
    keep, send = tile_call(
        forward_kernel,
        scalars,
        adjacency,
        (gathered,),
        (half, half),
        [pltpu.VMEM((CORES * owners, width, extent), jnp.float32)],
    )
    terms = (keep + lax.ppermute(send, "core", swap)).astype(jnp.bfloat16)
    terms = lax.all_to_all(
        terms.reshape(owners, width, extent), ("near", "feat"), 0, 0, tiled=False
    )
    outgoing, activated = pl.pallas_call(
        dense_kernel,
        out_shape=(
            jax.ShapeDtypeStruct((owners, width + PIECE, extent), jnp.bfloat16),
            jax.ShapeDtypeStruct((extent, full), jnp.bfloat16),
        ),
        in_specs=[VMEM_SPEC] * 3,
        out_specs=(VMEM_SPEC, VMEM_SPEC),
    )(terms.reshape(near, feats, width, extent), weight_all, grad_out)

    mine = lax.all_to_all(outgoing, ("near", "feat"), 0, 0, tiled=False)
    other = lax.ppermute(mine, "core", swap)
    pieces = tile_call(
        backward_kernel,
        scalars,
        adjacency,
        (mine, other),
        jax.ShapeDtypeStruct((rows, blocks * width + PIECE, extent), jnp.bfloat16),
        [
            pltpu.VMEM((near, CORES, feats, width, extent), jnp.bfloat16),
            pltpu.VMEM((rows * blocks, width, extent), jnp.float32),
        ],
    )
    pieces = lax.all_to_all(pieces, "row", 0, 0, tiled=False)
    scale = 1.0 / math.sqrt(nodes * rows * near * CORES)
    feature_grad, weight_piece = pl.pallas_call(
        lambda *refs: final_kernel(scale, *refs),
        out_shape=(
            jax.ShapeDtypeStruct((width, nodes), jnp.float32),
            jax.ShapeDtypeStruct((PIECE, extent), jnp.float32),
        ),
        in_specs=[VMEM_SPEC],
        out_specs=(VMEM_SPEC, VMEM_SPEC),
    )(pieces)
    weight_grad = lax.all_gather(weight_piece, "near", axis=0, tiled=True)
    weight_grad = weight_grad.reshape(width // PIECE, full // extent, PIECE, extent)
    weight_grad = weight_grad.transpose(0, 2, 1, 3).reshape(width, full)
    return (activated, weight_grad, feature_grad.T)


def solution(mesh):
    rows, cols, feats = (mesh.shape[name] for name in ("row", "col", "feat"))
    fine = jax.sharding.Mesh(
        mesh.devices.reshape(rows, cols // CORES, CORES, feats), ("row", "near", "core", "feat")
    )
    pair = P(("row", "near", "core"))
    owner = P(("row", "near", "core", "feat"), None)
    by_column = P(("near", "core", "row"), "feat")
    return jax.shard_map(
        local,
        mesh=fine,
        in_specs=(by_column, P("feat", None), owner, pair, pair, pair, pair),
        out_specs=(owner, P("feat", None), by_column),
        check_vma=False,
    )
```

```python
import math

import jax
import jax.numpy as jnp
from jax import lax
from jax.experimental import pallas as pl
from jax.experimental.pallas import tpu as pltpu
from jax.sharding import PartitionSpec as P

UNROLL = 8
PIECE = 16
CORES = 2
VMEM_LIMIT = 24 * 1024 * 1024
NT = (((1,), (1,)), ((), ()))
NN = (((1,), (0,)), ((), ()))
TN = (((0,), (0,)), ((), ()))


def dot(a, b, dims):
    return lax.dot_general(a, b, dims, preferred_element_type=jnp.float32)


def stage_kernel(source_ref, out_ref, done):
    copy = pltpu.make_async_copy(source_ref, out_ref, done)
    copy.start()
    copy.wait()


def accumulate_tiles(count, source, adj_ref, acc_ref, target_of, dims):
    acc_ref[...] = jnp.zeros_like(acc_ref)

    @pl.loop(0, adj_ref.shape[0] // UNROLL)
    def _(group):
        first = group * UNROLL

        @pl.when(first < count)
        def _():
            terms = []
            for u in range(UNROLL):
                term = dot(source(first + u), adj_ref[first + u], dims)
                terms.append(jnp.where(first + u < count, term, 0.0))
            for u in range(UNROLL):
                target = target_of(first + u)
                acc_ref[target] += terms[u]


def forward_kernel(core, rows, cols, count, adj_ref, feat_ref, keep_ref, send_ref, acc_ref):
    extent = adj_ref.shape[1]
    blocks = feat_ref.shape[2] // extent

    def source(slot):
        col = cols[slot]
        start = pl.multiple_of((col % blocks) * extent, extent)
        return feat_ref[col // blocks, :, pl.ds(start, extent)]

    accumulate_tiles(count[0], source, adj_ref, acc_ref, lambda s: rows[s], NT)
    near, feats = keep_ref.shape[:2]
    for pair in range(near):
        keep_ref[pair] = acc_ref[pl.ds((pair * CORES + core[0]) * feats, feats)]
        send_ref[pair] = acc_ref[pl.ds((pair * CORES + 1 - core[0]) * feats, feats)]


def spread_kernel(value_ref, out_ref):
    for copy in range(out_ref.shape[0]):
        out_ref[copy] = value_ref[...]


def combine_kernel(near, keep_ref, received_ref, weight_ref, out_ref):
    owners, width, extent = keep_ref.shape
    halves = weight_ref.shape[1] // extent
    out_ref[:, :width] = (keep_ref[...] + received_ref[...]).astype(out_ref.dtype)
    top = pl.multiple_of((near[0] // halves) * PIECE, PIECE)
    left = pl.multiple_of((near[0] % halves) * extent, extent)
    piece = weight_ref[pl.ds(top, PIECE), pl.ds(left, extent)]
    for owner in range(owners):
        out_ref[owner, width:] = piece


def dense_kernel(terms_ref, grad_ref, out_ref, act_ref, weight_ref):
    near, feats, height, extent = terms_ref.shape
    width = height - PIECE
    full = feats * width
    halves = full // extent
    for pair in range(near):
        for feat in range(feats):
            top = feat * width + (pair // halves) * PIECE
            left = (pair % halves) * extent
            weight_ref[top : top + PIECE, left : left + extent] = terms_ref[pair, feat, width:]
    weight = weight_ref[...]
    summed = jnp.sum(terms_ref[:, :, :width].astype(jnp.float32), axis=0).reshape(full, extent)
    high = summed.astype(jnp.bfloat16)
    low = (summed - high.astype(jnp.float32)).astype(jnp.bfloat16)
    pre_act = dot(high, weight, TN) + dot(low, weight, TN)
    gate = jax.nn.sigmoid(pre_act)
    act_ref[...] = (pre_act * gate).astype(act_ref.dtype)
    derivative = gate * (1.0 + pre_act * (1.0 - gate))
    grad_pre = (grad_ref[...] * derivative).astype(jnp.bfloat16)
    projected = dot(weight, grad_pre, NT).astype(out_ref.dtype)
    weight_term = (dot(high, grad_pre, NN) + dot(low, grad_pre, NN)).astype(out_ref.dtype)
    for pair in range(near):
        for feat in range(feats):
            top = feat * width + (pair // halves) * PIECE
            left = (pair % halves) * extent
            out_ref[pair * feats + feat, :width] = projected[feat * width : (feat + 1) * width]
            out_ref[pair * feats + feat, width:] = weight_term[
                top : top + PIECE, left : left + extent
            ]


def backward_kernel(
    core, rows, cols, count, adj_ref, mine_ref, other_ref, out_ref, proj_ref, acc_ref
):
    row_devices = out_ref.shape[0]
    blocks, width = acc_ref.shape[0] // row_devices, acc_ref.shape[1]
    feats = proj_ref.shape[2]
    for pair in range(proj_ref.shape[0]):
        part = slice(pair * feats, (pair + 1) * feats)
        proj_ref[pair, core[0]] = mine_ref[part, :width]
        proj_ref[pair, 1 - core[0]] = other_ref[part, :width]

    def source(slot):
        row = rows[slot]
        return proj_ref[row // (CORES * feats), (row // feats) % CORES, row % feats]

    accumulate_tiles(count[0], source, adj_ref, acc_ref, lambda s: cols[s], NN)
    weight_term = jnp.sum(mine_ref[:, width:].astype(jnp.float32), axis=0) + jnp.sum(
        other_ref[:, width:].astype(jnp.float32), axis=0
    )
    for row in range(row_devices):
        for block in range(blocks):
            out_ref[row, block * width : (block + 1) * width] = acc_ref[
                row * blocks + block
            ].astype(out_ref.dtype)
        out_ref[row, blocks * width :] = weight_term.astype(out_ref.dtype)


def final_kernel(scale, pieces_ref, grad_ref, weight_ref):
    width, nodes = grad_ref.shape
    extent = pieces_ref.shape[2]
    for block in range(nodes // extent):
        grad_ref[:, block * extent : (block + 1) * extent] = jnp.sum(
            pieces_ref[:, block * width : (block + 1) * width].astype(jnp.float32), axis=0
        )
    rest = pieces_ref[:, nodes // extent * width :].astype(jnp.float32)
    weight_term = jnp.sum(rest, axis=0) * scale
    for pair in range(weight_ref.shape[0]):
        weight_ref[pair] = weight_term


SMEM_SPEC = pl.BlockSpec(memory_space=pltpu.SMEM)
VMEM_SPEC = pl.BlockSpec(memory_space=pltpu.VMEM)


def stage(array):
    return pl.pallas_call(
        stage_kernel,
        out_shape=pltpu.VMEM(array.shape, array.dtype),
        in_specs=[pl.BlockSpec(memory_space=pltpu.HBM)],
        out_specs=VMEM_SPEC,
        scratch_shapes=[pltpu.SemaphoreType.DMA],
        compiler_params=pltpu.CompilerParams(vmem_limit_bytes=VMEM_LIMIT),
        cost_estimate=pl.CostEstimate(
            flops=0, bytes_accessed=2 * array.size * 2, transcendentals=0
        ),
    )(pltpu.with_memory_space_constraint(array, pltpu.HBM))


def in_vmem(array):
    return pltpu.with_memory_space_constraint(array, pltpu.VMEM)


def call(kernel, scalars, arrays, out_shapes, scratch=()):
    return pl.pallas_call(
        kernel,
        out_shape=out_shapes,
        in_specs=[SMEM_SPEC] * len(scalars) + [VMEM_SPEC] * len(arrays),
        out_specs=jax.tree.map(lambda _: VMEM_SPEC, out_shapes),
        scratch_shapes=scratch,
        compiler_params=pltpu.CompilerParams(vmem_limit_bytes=VMEM_LIMIT),
    )(*scalars, *(in_vmem(array) for array in arrays))


def local(features, weight, grad_out, adjacency, tile_rows, tile_cols, tile_count):
    nodes, width = features.shape
    extent = adjacency.shape[1]
    rows, near, feats = (lax.axis_size(name) for name in ("row", "near", "feat"))
    full = feats * width
    blocks = nodes // extent
    owners = near * feats
    swap = [(i, CORES - 1 - i) for i in range(CORES)]
    core, near_index = (
        lax.axis_index(name).astype(jnp.int32).reshape(1) for name in ("core", "near")
    )
    scalars = (core, tile_rows, tile_cols, tile_count)
    bf16, f32 = jnp.bfloat16, jnp.float32

    own = call(spread_kernel, (), (features.T,), pltpu.VMEM((rows, width, nodes), bf16))
    gathered = lax.all_to_all(own, "row", 0, 0, tiled=False)
    tiles = stage(adjacency)

    half = jax.ShapeDtypeStruct((near, feats, width, extent), f32)
    keep, send = call(
        forward_kernel,
        scalars,
        (tiles, gathered),
        (half, half),
        [pltpu.VMEM((CORES * owners, width, extent), f32)],
    )
    received = lax.ppermute(send, "core", swap)
    flat = (owners, width, extent)
    terms = call(
        combine_kernel,
        (near_index,),
        (keep.reshape(flat), received.reshape(flat), weight),
        pltpu.VMEM((owners, width + PIECE, extent), bf16),
    )
    terms, grad_out = lax.optimization_barrier((terms, grad_out))
    terms = lax.all_to_all(terms, ("near", "feat"), 0, 0, tiled=False)
    outgoing, activated = call(
        dense_kernel,
        (),
        (terms.reshape(near, feats, width + PIECE, extent), grad_out.astype(f32)),
        (
            pltpu.VMEM((owners, width + PIECE, extent), bf16),
            jax.ShapeDtypeStruct((extent, full), f32),
        ),
        [pltpu.VMEM((full, full), bf16)],
    )

    outgoing, adjacency = lax.optimization_barrier((outgoing, adjacency))
    mine = lax.all_to_all(outgoing, ("near", "feat"), 0, 0, tiled=False)
    tiles = stage(adjacency)
    other = lax.ppermute(mine, "core", swap)
    pieces = call(
        backward_kernel,
        scalars,
        (tiles, mine, other),
        pltpu.VMEM((rows, blocks * width + PIECE, extent), bf16),
        [
            pltpu.VMEM((near, CORES, feats, width, extent), bf16),
            pltpu.VMEM((rows * blocks, width, extent), f32),
        ],
    )
    pieces, activated = lax.optimization_barrier((pieces, activated))
    pieces = lax.all_to_all(pieces, "row", 0, 0, tiled=False)
    activated = activated.astype(bf16)
    scale = 1.0 / math.sqrt(nodes * rows * near * CORES)
    feature_grad, weight_piece = call(
        lambda *refs: final_kernel(scale, *refs),
        (),
        (pieces,),
        (
            jax.ShapeDtypeStruct((width, nodes), f32),
            pltpu.VMEM((near, PIECE, extent), f32),
        ),
    )
    weight_grad = lax.all_to_all(weight_piece, "near", 0, 0, tiled=False)
    weight_grad = weight_grad.reshape(width // PIECE, full // extent, PIECE, extent)
    weight_grad = weight_grad.transpose(0, 2, 1, 3).reshape(width, full)
    return (activated, weight_grad, feature_grad.T)


def solution(mesh):
    rows, cols, feats = (mesh.shape[name] for name in ("row", "col", "feat"))
    fine = jax.sharding.Mesh(
        mesh.devices.reshape(rows, cols // CORES, CORES, feats), ("row", "near", "core", "feat")
    )
    pair = P(("row", "near", "core"))
    owner = P(("row", "near", "core", "feat"), None)
    by_column = P(("near", "core", "row"), "feat")
    return jax.shard_map(
        local,
        mesh=fine,
        in_specs=(by_column, P("feat", None), owner, pair, pair, pair, pair),
        out_specs=(owner, P("feat", None), by_column),
        check_vma=False,
    )
```

```python
import math

import jax
import jax.numpy as jnp
from jax import lax
from jax.experimental import pallas as pl
from jax.experimental.pallas import tpu as pltpu
from jax.sharding import PartitionSpec as P

UNROLL = 8
CHUNK = 16
PIECE = 16
CORES = 2
SIDES = 2
VMEM_LIMIT = 24 * 1024 * 1024
NT = (((1,), (1,)), ((), ()))
NN = (((1,), (0,)), ((), ()))
TN = (((0,), (0,)), ((), ()))


def dot(a, b, dims):
    return lax.dot_general(a, b, dims, preferred_element_type=jnp.float32)


def accumulate_tiles(count, source, adj_ref, tiles_ref, done, acc_ref, target_of, dims):
    chunks = adj_ref.shape[0] // CHUNK

    def load(chunk):
        part = pl.ds(chunk * CHUNK, CHUNK)
        return pltpu.make_async_copy(adj_ref.at[part], tiles_ref.at[part], done.at[chunk])

    for chunk in range(chunks):
        load(chunk).start()
    acc_ref[...] = jnp.zeros_like(acc_ref)

    @pl.loop(0, chunks)
    def _(chunk):
        load(chunk).wait()

        @pl.loop(0, CHUNK // UNROLL)
        def _(group):
            first = chunk * CHUNK + group * UNROLL

            @pl.when(first < count)
            def _():
                terms = []
                for u in range(UNROLL):
                    term = dot(source(first + u), tiles_ref[first + u], dims)
                    terms.append(jnp.where(first + u < count, term, 0.0))
                for u in range(UNROLL):
                    target = target_of(first + u)
                    acc_ref[target] += terms[u]


def forward_kernel(
    place, rows, cols, count, adj_ref, same_ref, far_ref, keep_ref, send_ref, acc_ref, *tiles
):
    core, side = place[0], place[1]
    extent = adj_ref.shape[1]
    blocks = same_ref.shape[2] // extent

    def source(slot):
        col = cols[slot]
        row_device = col // blocks
        nodes = pl.ds(pl.multiple_of((col % blocks) * extent, extent), extent)
        ring = row_device // SIDES
        return jnp.where(
            row_device % SIDES == side, same_ref[ring, :, nodes], far_ref[ring, :, nodes]
        )

    accumulate_tiles(count[0], source, adj_ref, *tiles, acc_ref, lambda s: rows[s], NT)
    near, feats = keep_ref.shape[:2]
    for pair in range(near):
        keep_ref[pair] = acc_ref[pl.ds((pair * CORES + core) * feats, feats)]
        send_ref[pair] = acc_ref[pl.ds((pair * CORES + 1 - core) * feats, feats)]


def spread_kernel(value_ref, out_ref):
    for copy in range(out_ref.shape[0]):
        out_ref[copy] = value_ref[...]


def combine_kernel(near, keep_ref, received_ref, weight_ref, out_ref):
    owners, width, extent = keep_ref.shape
    halves = weight_ref.shape[1] // extent
    out_ref[:, :width] = (keep_ref[...] + received_ref[...]).astype(out_ref.dtype)
    top = pl.multiple_of((near[0] // halves) * PIECE, PIECE)
    left = pl.multiple_of((near[0] % halves) * extent, extent)
    piece = weight_ref[pl.ds(top, PIECE), pl.ds(left, extent)]
    for owner in range(owners):
        out_ref[owner, width:] = piece


def dense_kernel(terms_ref, grad_ref, out_ref, act_ref, weight_ref):
    near, feats, height, extent = terms_ref.shape
    width = height - PIECE
    full = feats * width
    halves = full // extent
    for pair in range(near):
        for feat in range(feats):
            top = feat * width + (pair // halves) * PIECE
            left = (pair % halves) * extent
            weight_ref[top : top + PIECE, left : left + extent] = terms_ref[pair, feat, width:]
    weight = weight_ref[...]
    summed = jnp.sum(terms_ref[:, :, :width].astype(jnp.float32), axis=0).reshape(full, extent)
    high = summed.astype(jnp.bfloat16)
    low = (summed - high.astype(jnp.float32)).astype(jnp.bfloat16)
    pre_act = dot(high, weight, TN) + dot(low, weight, TN)
    gate = jax.nn.sigmoid(pre_act)
    act_ref[...] = (pre_act * gate).astype(act_ref.dtype)
    derivative = gate * (1.0 + pre_act * (1.0 - gate))
    grad_pre = (grad_ref[...].astype(jnp.float32) * derivative).astype(jnp.bfloat16)
    projected = dot(weight, grad_pre, NT).astype(out_ref.dtype)
    weight_term = (dot(high, grad_pre, NN) + dot(low, grad_pre, NN)).astype(out_ref.dtype)
    for pair in range(near):
        for feat in range(feats):
            top = feat * width + (pair // halves) * PIECE
            left = (pair % halves) * extent
            out_ref[pair * feats + feat, :width] = projected[feat * width : (feat + 1) * width]
            out_ref[pair * feats + feat, width:] = weight_term[
                top : top + PIECE, left : left + extent
            ]


def backward_kernel(
    place, rows, cols, count, adj_ref, mine_ref, other_ref, far_ref, same_ref, proj_ref, acc_ref, *tiles
):
    core, side = place[0], place[1]
    rings = far_ref.shape[0]
    width = acc_ref.shape[1]
    blocks = acc_ref.shape[0] // (rings * SIDES)
    feats = proj_ref.shape[2]
    for pair in range(proj_ref.shape[0]):
        part = slice(pair * feats, (pair + 1) * feats)
        proj_ref[pair, core] = mine_ref[part, :width]
        proj_ref[pair, 1 - core] = other_ref[part, :width]

    def source(slot):
        row = rows[slot]
        return proj_ref[row // (CORES * feats), (row // feats) % CORES, row % feats]

    accumulate_tiles(count[0], source, adj_ref, *tiles, acc_ref, lambda s: cols[s], NN)
    weight_term = jnp.sum(mine_ref[:, width:].astype(jnp.float32), axis=0) + jnp.sum(
        other_ref[:, width:].astype(jnp.float32), axis=0
    )
    for ring in range(rings):
        for out_ref, out_side in ((far_ref, 1 - side), (same_ref, side)):
            start = (ring * SIDES + out_side) * blocks
            for block in range(blocks):
                out_ref[ring, block * width : (block + 1) * width] = acc_ref[start + block].astype(
                    out_ref.dtype
                )
        far_ref[ring, blocks * width :] = weight_term.astype(far_ref.dtype)


def reduce_kernel(pieces_ref, out_ref):
    out_ref[...] = jnp.sum(pieces_ref[...].astype(jnp.float32), axis=0)


def final_kernel(scale, same_ref, swapped_ref, summed_ref, grad_ref, weight_ref):
    width, nodes = grad_ref.shape
    extent = same_ref.shape[2]
    for block in range(nodes // extent):
        part = slice(block * width, (block + 1) * width)
        grad_ref[:, block * extent : (block + 1) * extent] = swapped_ref[part] + jnp.sum(
            same_ref[:, part].astype(jnp.float32), axis=0
        )
    rest = slice(nodes // extent * width, None)
    weight_term = (summed_ref[rest] + swapped_ref[rest]) * scale
    for pair in range(weight_ref.shape[0]):
        weight_ref[pair] = weight_term


SMEM_SPEC = pl.BlockSpec(memory_space=pltpu.SMEM)
VMEM_SPEC = pl.BlockSpec(memory_space=pltpu.VMEM)


def in_vmem(array):
    return pltpu.with_memory_space_constraint(array, pltpu.VMEM)


def call(kernel, scalars, arrays, out_shapes, scratch=()):
    return pl.pallas_call(
        kernel,
        out_shape=out_shapes,
        in_specs=[SMEM_SPEC] * len(scalars) + [VMEM_SPEC] * len(arrays),
        out_specs=jax.tree.map(lambda _: VMEM_SPEC, out_shapes),
        scratch_shapes=scratch,
        compiler_params=pltpu.CompilerParams(vmem_limit_bytes=VMEM_LIMIT),
    )(*scalars, *(in_vmem(array) for array in arrays))


def tile_call(kernel, scalars, adjacency, arrays, out_shapes, scratch):
    return pl.pallas_call(
        kernel,
        out_shape=out_shapes,
        in_specs=[SMEM_SPEC] * len(scalars)
        + [pl.BlockSpec(memory_space=pltpu.HBM)]
        + [VMEM_SPEC] * len(arrays),
        out_specs=jax.tree.map(lambda _: VMEM_SPEC, out_shapes),
        scratch_shapes=[
            *scratch,
            pltpu.VMEM(adjacency.shape, adjacency.dtype),
            pltpu.SemaphoreType.DMA((adjacency.shape[0] // CHUNK,)),
        ],
        compiler_params=pltpu.CompilerParams(vmem_limit_bytes=VMEM_LIMIT),
    )(
        *scalars,
        pltpu.with_memory_space_constraint(adjacency, pltpu.HBM),
        *(in_vmem(array) for array in arrays),
    )


def local(features, weight, grad_out, adjacency, tile_rows, tile_cols, tile_count):
    nodes, width = features.shape
    extent = adjacency.shape[1]
    rings, near, feats = (lax.axis_size(name) for name in ("ring", "near", "feat"))
    full = feats * width
    blocks = nodes // extent
    owners = near * feats
    swap = [(0, 1), (1, 0)]
    core, side, near_index = (
        lax.axis_index(name).astype(jnp.int32) for name in ("core", "side", "near")
    )
    scalars = (jnp.stack([core, side]), tile_rows, tile_cols, tile_count)
    bf16, f32 = jnp.bfloat16, jnp.float32

    def spread(value):
        copies = call(spread_kernel, (), (value,), pltpu.VMEM((rings, width, nodes), bf16))
        return lax.all_to_all(copies, "ring", 0, 0, tiled=False)

    own = features.T
    partner = lax.ppermute(own, "side", swap)
    same = spread(own)
    same, partner = lax.optimization_barrier((same, partner))
    far = spread(partner)

    half = jax.ShapeDtypeStruct((near, feats, width, extent), f32)
    keep, send = tile_call(
        forward_kernel,
        scalars,
        adjacency,
        (same, far),
        (half, half),
        [pltpu.VMEM((CORES * owners, width, extent), f32)],
    )
    received = lax.ppermute(send, "core", swap)
    flat = (owners, width, extent)
    terms = call(
        combine_kernel,
        (near_index.reshape(1),),
        (keep.reshape(flat), received.reshape(flat), weight),
        pltpu.VMEM((owners, width + PIECE, extent), bf16),
    )
    terms = lax.all_to_all(terms, ("near", "feat"), 0, 0, tiled=False)
    outgoing, activated = call(
        dense_kernel,
        (),
        (terms.reshape(near, feats, width + PIECE, extent), grad_out),
        (
            pltpu.VMEM((owners, width + PIECE, extent), bf16),
            jax.ShapeDtypeStruct((extent, full), bf16),
        ),
        [pltpu.VMEM((full, full), bf16)],
    )

    mine = lax.all_to_all(outgoing, ("near", "feat"), 0, 0, tiled=False)
    other = lax.ppermute(mine, "core", swap)
    far, same = tile_call(
        backward_kernel,
        scalars,
        adjacency,
        (mine, other),
        (
            pltpu.VMEM((rings, blocks * width + PIECE, extent), bf16),
            pltpu.VMEM((rings, blocks * width, extent), bf16),
        ),
        [
            pltpu.VMEM((near, CORES, feats, width, extent), bf16),
            pltpu.VMEM((rings * SIDES * blocks, width, extent), f32),
        ],
    )
    far = lax.all_to_all(far, "ring", 0, 0, tiled=False)
    summed = call(
        reduce_kernel,
        (),
        (far,),
        jax.ShapeDtypeStruct((blocks * width + PIECE, extent), f32),
    )
    swapped = lax.ppermute(summed, "side", swap)
    same, summed = lax.optimization_barrier((same, summed))
    same = lax.all_to_all(same, "ring", 0, 0, tiled=False)
    scale = 1.0 / math.sqrt(nodes * rings * SIDES * near * CORES)
    feature_grad, weight_piece = call(
        lambda *refs: final_kernel(scale, *refs),
        (),
        (same, swapped, summed),
        (
            jax.ShapeDtypeStruct((width, nodes), f32),
            pltpu.VMEM((near, PIECE, extent), f32),
        ),
    )
    weight_grad = lax.all_to_all(weight_piece, "near", 0, 0, tiled=False)
    weight_grad = weight_grad.reshape(width // PIECE, full // extent, PIECE, extent)
    weight_grad = weight_grad.transpose(0, 2, 1, 3).reshape(width, full)
    return (activated, weight_grad, feature_grad.T)


def solution(mesh):
    rows, cols, feats = (mesh.shape[name] for name in ("row", "col", "feat"))
    fine = jax.sharding.Mesh(
        mesh.devices.reshape(rows // SIDES, SIDES, cols // CORES, CORES, feats),
        ("ring", "side", "near", "core", "feat"),
    )
    pair = P(("ring", "side", "near", "core"))
    owner = P(("ring", "side", "near", "core", "feat"), None)
    by_column = P(("near", "core", "ring", "side"), "feat")
    return jax.shard_map(
        local,
        mesh=fine,
        in_specs=(by_column, P("feat", None), owner, pair, pair, pair, pair),
        out_specs=(owner, P("feat", None), by_column),
        check_vma=False,
    )
```

```python
import math

import jax
import jax.numpy as jnp
from jax import lax
from jax.experimental import pallas as pl
from jax.experimental.pallas import tpu as pltpu
from jax.sharding import PartitionSpec as P

UNROLL = 8
CHUNK = 16
PIECE = 16
CORES = 2
SIDES = 2
HEAD = 3
VMEM_LIMIT = 24 * 1024 * 1024
NT = (((1,), (1,)), ((), ()))
NN = (((1,), (0,)), ((), ()))
TN = (((0,), (0,)), ((), ()))


def dot(a, b, dims):
    return lax.dot_general(a, b, dims, preferred_element_type=jnp.float32)


def accumulate_tiles(count, source, adj_ref, tiles_ref, done, acc_ref, target_of, dims):
    chunks = adj_ref.shape[0] // CHUNK

    def load(chunk):
        part = pl.ds(chunk * CHUNK, CHUNK)
        return pltpu.make_async_copy(adj_ref.at[part], tiles_ref.at[part], done.at[chunk])

    for chunk in range(chunks):
        load(chunk).start()
    acc_ref[...] = jnp.zeros_like(acc_ref)

    @pl.loop(0, chunks)
    def _(chunk):
        load(chunk).wait()

        @pl.loop(0, CHUNK // UNROLL)
        def _(group):
            first = chunk * CHUNK + group * UNROLL

            @pl.when(first < count)
            def _():
                terms = []
                for u in range(UNROLL):
                    term = dot(source(first + u), tiles_ref[first + u], dims)
                    terms.append(jnp.where(first + u < count, term, 0.0))
                for u in range(UNROLL):
                    target = target_of(first + u)
                    acc_ref[target] += terms[u]


def slots_of(table, slots):
    return lambda s: table[HEAD + s], lambda s: table[HEAD + slots + s]


def forward_kernel(table, adj_ref, feat_ref, keep_ref, send_ref, acc_ref, *tiles):
    core, count = table[0], table[2]
    slots, extent, _ = adj_ref.shape
    blocks = feat_ref.shape[2] // extent
    row_of, col_of = slots_of(table, slots)

    def source(slot):
        col = col_of(slot)
        nodes = pl.ds(pl.multiple_of((col % blocks) * extent, extent), extent)
        return feat_ref[col // blocks, :, nodes]

    accumulate_tiles(count, source, adj_ref, *tiles, acc_ref, row_of, NT)
    near, feats = keep_ref.shape[:2]
    for pair in range(near):
        keep_ref[pair] = acc_ref[pl.ds((pair * CORES + core) * feats, feats)]
        send_ref[pair] = acc_ref[pl.ds((pair * CORES + 1 - core) * feats, feats)]


def spread_kernel(value_ref, out_ref):
    for copy in range(out_ref.shape[0]):
        out_ref[copy] = value_ref[...]


def combine_kernel(near, keep_ref, received_ref, weight_ref, out_ref):
    owners, width, extent = keep_ref.shape
    halves = weight_ref.shape[1] // extent
    out_ref[:, :width] = (keep_ref[...] + received_ref[...]).astype(out_ref.dtype)
    top = pl.multiple_of((near[0] // halves) * PIECE, PIECE)
    left = pl.multiple_of((near[0] % halves) * extent, extent)
    piece = weight_ref[pl.ds(top, PIECE), pl.ds(left, extent)]
    for owner in range(owners):
        out_ref[owner, width:] = piece


def dense_kernel(terms_ref, grad_ref, out_ref, act_ref, weight_ref):
    near, feats, height, extent = terms_ref.shape
    width = height - PIECE
    full = feats * width
    halves = full // extent
    for pair in range(near):
        for feat in range(feats):
            top = feat * width + (pair // halves) * PIECE
            left = (pair % halves) * extent
            weight_ref[top : top + PIECE, left : left + extent] = terms_ref[pair, feat, width:]
    weight = weight_ref[...]
    summed = jnp.sum(terms_ref[:, :, :width].astype(jnp.float32), axis=0).reshape(full, extent)
    high = summed.astype(jnp.bfloat16)
    low = (summed - high.astype(jnp.float32)).astype(jnp.bfloat16)
    pre_act = dot(high, weight, TN) + dot(low, weight, TN)
    gate = jax.nn.sigmoid(pre_act)
    act_ref[...] = (pre_act * gate).astype(act_ref.dtype)
    derivative = gate * (1.0 + pre_act * (1.0 - gate))
    grad_pre = (grad_ref[...].astype(jnp.float32) * derivative).astype(jnp.bfloat16)
    projected = dot(weight, grad_pre, NT).astype(out_ref.dtype)
    weight_term = (dot(high, grad_pre, NN) + dot(low, grad_pre, NN)).astype(out_ref.dtype)
    for pair in range(near):
        for feat in range(feats):
            out_ref[pair * feats + feat, :width] = projected[feat * width : (feat + 1) * width]
            for part in range((out_ref.shape[1] - width) // PIECE):
                top = feat * width + (part // halves) * PIECE
                left = (part % halves) * extent
                out_ref[
                    pair * feats + feat, width + part * PIECE : width + (part + 1) * PIECE
                ] = weight_term[top : top + PIECE, left : left + extent]


def backward_kernel(
    table, adj_ref, mine_ref, other_ref, far_ref, same_ref, proj_ref, acc_ref, *tiles
):
    core, side, count = table[0], table[1], table[2]
    row_of, col_of = slots_of(table, adj_ref.shape[0])
    rings = far_ref.shape[0]
    width = acc_ref.shape[1]
    blocks = acc_ref.shape[0] // (rings * SIDES)
    feats = proj_ref.shape[2]
    for pair in range(proj_ref.shape[0]):
        part = slice(pair * feats, (pair + 1) * feats)
        proj_ref[pair, core] = mine_ref[part, :width]
        proj_ref[pair, 1 - core] = other_ref[part, :width]

    def source(slot):
        row = row_of(slot)
        return proj_ref[row // (CORES * feats), (row // feats) % CORES, row % feats]

    accumulate_tiles(count, source, adj_ref, *tiles, acc_ref, col_of, NN)
    weight_term = jnp.sum(mine_ref[:, width:].astype(jnp.float32), axis=0) + jnp.sum(
        other_ref[:, width:].astype(jnp.float32), axis=0
    )
    for ring in range(rings):
        for out_ref, out_side in ((far_ref, 1 - side), (same_ref, side)):
            start = (ring * SIDES + out_side) * blocks
            for block in range(blocks):
                out_ref[ring, block * width : (block + 1) * width] = acc_ref[start + block].astype(
                    out_ref.dtype
                )
        far_ref[ring, blocks * width :] = weight_term.astype(far_ref.dtype)


def reduce_kernel(pieces_ref, out_ref):
    out_ref[...] = jnp.sum(pieces_ref[...].astype(jnp.float32), axis=0)


def final_kernel(scale, same_ref, swapped_ref, summed_ref, grad_ref, weight_ref):
    width, nodes = grad_ref.shape
    extent = same_ref.shape[2]
    for block in range(nodes // extent):
        part = slice(block * width, (block + 1) * width)
        grad_ref[:, block * extent : (block + 1) * extent] = swapped_ref[part] + jnp.sum(
            same_ref[:, part].astype(jnp.float32), axis=0
        )
    halves = weight_ref.shape[1] // extent
    for part in range(width // PIECE * halves):
        start = nodes // extent * width + part * PIECE
        rest = slice(start, start + PIECE)
        top, left = (part // halves) * PIECE, (part % halves) * extent
        weight_ref[top : top + PIECE, left : left + extent] = (
            summed_ref[rest] + swapped_ref[rest]
        ) * scale


SMEM_SPEC = pl.BlockSpec(memory_space=pltpu.SMEM)
VMEM_SPEC = pl.BlockSpec(memory_space=pltpu.VMEM)


def in_vmem(array):
    return pltpu.with_memory_space_constraint(array, pltpu.VMEM)


def call(kernel, scalars, arrays, out_shapes, scratch=()):
    return pl.pallas_call(
        kernel,
        out_shape=out_shapes,
        in_specs=[SMEM_SPEC] * len(scalars) + [VMEM_SPEC] * len(arrays),
        out_specs=jax.tree.map(lambda _: VMEM_SPEC, out_shapes),
        scratch_shapes=scratch,
        compiler_params=pltpu.CompilerParams(vmem_limit_bytes=VMEM_LIMIT),
    )(*scalars, *(in_vmem(array) for array in arrays))


def tile_call(kernel, scalars, adjacency, arrays, out_shapes, scratch):
    return pl.pallas_call(
        kernel,
        out_shape=out_shapes,
        in_specs=[SMEM_SPEC] * len(scalars)
        + [pl.BlockSpec(memory_space=pltpu.HBM)]
        + [VMEM_SPEC] * len(arrays),
        out_specs=jax.tree.map(lambda _: VMEM_SPEC, out_shapes),
        scratch_shapes=[
            *scratch,
            pltpu.VMEM(adjacency.shape, adjacency.dtype),
            pltpu.SemaphoreType.DMA((adjacency.shape[0] // CHUNK,)),
        ],
        compiler_params=pltpu.CompilerParams(vmem_limit_bytes=VMEM_LIMIT),
    )(
        *scalars,
        pltpu.with_memory_space_constraint(adjacency, pltpu.HBM),
        *(in_vmem(array) for array in arrays),
    )


def local(features, weight, grad_out, adjacency, tile_rows, tile_cols, tile_count):
    nodes, width = features.shape
    extent = adjacency.shape[1]
    rings, near, feats = (lax.axis_size(name) for name in ("ring", "near", "feat"))
    full = feats * width
    blocks = nodes // extent
    owners = near * feats
    swap = [(0, 1), (1, 0)]
    core, side, near_index = (
        lax.axis_index(name).astype(jnp.int32) for name in ("core", "side", "near")
    )
    table = jnp.concatenate([jnp.stack([core, side]), tile_count, tile_rows, tile_cols])
    parts = full // extent * width // PIECE
    bf16, f32 = jnp.bfloat16, jnp.float32

    own = call(
        spread_kernel, (), (features.T,), pltpu.VMEM((rings * SIDES, width, nodes), bf16)
    )
    gathered = lax.all_to_all(own, ("ring", "side"), 0, 0, tiled=False)

    half = jax.ShapeDtypeStruct((near, feats, width, extent), f32)
    keep, send = tile_call(
        forward_kernel,
        (table,),
        adjacency,
        (gathered,),
        (half, half),
        [pltpu.VMEM((CORES * owners, width, extent), f32)],
    )
    received = lax.ppermute(send, "core", swap)
    flat = (owners, width, extent)
    terms = call(
        combine_kernel,
        (near_index.reshape(1),),
        (keep.reshape(flat), received.reshape(flat), weight),
        pltpu.VMEM((owners, width + PIECE, extent), bf16),
    )
    terms = lax.all_to_all(terms, ("near", "feat"), 0, 0, tiled=False)
    outgoing, activated = call(
        dense_kernel,
        (),
        (terms.reshape(near, feats, width + PIECE, extent), grad_out),
        (
            pltpu.VMEM((owners, width + parts * PIECE, extent), bf16),
            jax.ShapeDtypeStruct((extent, full), bf16),
        ),
        [pltpu.VMEM((full, full), bf16)],
    )

    mine = lax.all_to_all(outgoing, ("near", "feat"), 0, 0, tiled=False)
    other = lax.ppermute(mine, "core", swap)
    far, same = tile_call(
        backward_kernel,
        (table,),
        adjacency,
        (mine, other),
        (
            pltpu.VMEM((rings, blocks * width + parts * PIECE, extent), bf16),
            pltpu.VMEM((rings, blocks * width, extent), bf16),
        ),
        [
            pltpu.VMEM((near, CORES, feats, width, extent), bf16),
            pltpu.VMEM((rings * SIDES * blocks, width, extent), f32),
        ],
    )
    far = lax.all_to_all(far, "ring", 0, 0, tiled=False)
    summed = call(
        reduce_kernel,
        (),
        (far,),
        jax.ShapeDtypeStruct((blocks * width + parts * PIECE, extent), f32),
    )
    swapped = lax.ppermute(summed, "side", swap)
    same, summed = lax.optimization_barrier((same, summed))
    same = lax.all_to_all(same, "ring", 0, 0, tiled=False)
    scale = 1.0 / math.sqrt(nodes * rings * SIDES * near * CORES)
    feature_grad, weight_grad = call(
        lambda *refs: final_kernel(scale, *refs),
        (),
        (same, swapped, summed),
        (
            jax.ShapeDtypeStruct((width, nodes), f32),
            jax.ShapeDtypeStruct((width, full), f32),
        ),
    )
    return (activated, weight_grad, feature_grad.T)


def solution(mesh):
    rows, cols, feats = (mesh.shape[name] for name in ("row", "col", "feat"))
    fine = jax.sharding.Mesh(
        mesh.devices.reshape(rows // SIDES, SIDES, cols // CORES, CORES, feats),
        ("ring", "side", "near", "core", "feat"),
    )
    pair = P(("ring", "side", "near", "core"))
    owner = P(("ring", "side", "near", "core", "feat"), None)
    by_column = P(("near", "core", "ring", "side"), "feat")
    return jax.shard_map(
        local,
        mesh=fine,
        in_specs=(by_column, P("feat", None), owner, pair, pair, pair, pair),
        out_specs=(owner, P("feat", None), by_column),
        check_vma=False,
    )
```

```python
import math

import jax
import jax.numpy as jnp
from jax import lax
from jax.experimental import pallas as pl
from jax.experimental.pallas import tpu as pltpu
from jax.sharding import PartitionSpec as P

UNROLL = 8
CHUNK = 16
PIECE = 16
CORES = 2
SIDES = 2
HEAD = 3
VMEM_LIMIT = 24 * 1024 * 1024
NT = (((1,), (1,)), ((), ()))
NN = (((1,), (0,)), ((), ()))
TN = (((0,), (0,)), ((), ()))


def dot(a, b, dims):
    return lax.dot_general(a, b, dims, preferred_element_type=jnp.float32)


def accumulate_tiles(count, source, adj_ref, tiles_ref, done, acc_ref, target_of, dims):
    chunks = adj_ref.shape[0] // CHUNK

    def load(chunk):
        part = pl.ds(chunk * CHUNK, CHUNK)
        return pltpu.make_async_copy(adj_ref.at[part], tiles_ref.at[part], done.at[chunk])

    for chunk in range(chunks):
        load(chunk).start()
    acc_ref[...] = jnp.zeros_like(acc_ref)

    @pl.loop(0, chunks)
    def _(chunk):
        load(chunk).wait()

        @pl.loop(0, CHUNK // UNROLL)
        def _(group):
            first = chunk * CHUNK + group * UNROLL

            @pl.when(first < count)
            def _():
                terms = []
                for u in range(UNROLL):
                    term = dot(source(first + u), tiles_ref[first + u], dims)
                    terms.append(jnp.where(first + u < count, term, 0.0))
                for u in range(UNROLL):
                    target = target_of(first + u)
                    acc_ref[target] += terms[u]


def slots_of(table, slots):
    return lambda s: table[HEAD + s], lambda s: table[HEAD + slots + s]


def forward_kernel(table, adj_ref, same_ref, far_ref, keep_ref, send_ref, acc_ref, *tiles):
    core, side, count = table[0], table[1], table[2]
    slots, extent, _ = adj_ref.shape
    blocks = same_ref.shape[2] // extent
    row_of, col_of = slots_of(table, slots)

    def source(slot):
        col = col_of(slot)
        row_device = col // blocks
        nodes = pl.ds(pl.multiple_of((col % blocks) * extent, extent), extent)
        ring = row_device // SIDES
        return jnp.where(
            row_device % SIDES == side, same_ref[ring, :, nodes], far_ref[ring, :, nodes]
        )

    accumulate_tiles(count, source, adj_ref, *tiles, acc_ref, row_of, NT)
    near, feats = keep_ref.shape[:2]
    for pair in range(near):
        keep_ref[pair] = acc_ref[pl.ds((pair * CORES + core) * feats, feats)]
        send_ref[pair] = acc_ref[pl.ds((pair * CORES + 1 - core) * feats, feats)]


def spread_kernel(value_ref, out_ref):
    for copy in range(out_ref.shape[0]):
        out_ref[copy] = value_ref[...]


def combine_kernel(near, keep_ref, received_ref, weight_ref, out_ref):
    owners, width, extent = keep_ref.shape
    halves = weight_ref.shape[1] // extent
    out_ref[:, :width] = (keep_ref[...] + received_ref[...]).astype(out_ref.dtype)
    top = pl.multiple_of((near[0] // halves) * PIECE, PIECE)
    left = pl.multiple_of((near[0] % halves) * extent, extent)
    piece = weight_ref[pl.ds(top, PIECE), pl.ds(left, extent)]
    for owner in range(owners):
        out_ref[owner, width:] = piece


def dense_kernel(terms_ref, grad_ref, out_ref, act_ref, weight_ref):
    near, feats, height, extent = terms_ref.shape
    width = height - PIECE
    full = feats * width
    halves = full // extent
    for pair in range(near):
        for feat in range(feats):
            top = feat * width + (pair // halves) * PIECE
            left = (pair % halves) * extent
            weight_ref[top : top + PIECE, left : left + extent] = terms_ref[pair, feat, width:]
    weight = weight_ref[...]
    summed = jnp.sum(terms_ref[:, :, :width].astype(jnp.float32), axis=0).reshape(full, extent)
    high = summed.astype(jnp.bfloat16)
    low = (summed - high.astype(jnp.float32)).astype(jnp.bfloat16)
    pre_act = dot(high, weight, TN) + dot(low, weight, TN)
    gate = jax.nn.sigmoid(pre_act)
    act_ref[...] = (pre_act * gate).astype(act_ref.dtype)
    derivative = gate * (1.0 + pre_act * (1.0 - gate))
    grad_pre = (grad_ref[...].astype(jnp.float32) * derivative).astype(jnp.bfloat16)
    projected = dot(weight, grad_pre, NT).astype(out_ref.dtype)
    weight_term = (dot(high, grad_pre, NN) + dot(low, grad_pre, NN)).astype(out_ref.dtype)
    for pair in range(near):
        for feat in range(feats):
            top = feat * width + (pair // halves) * PIECE
            left = (pair % halves) * extent
            out_ref[pair * feats + feat, :width] = projected[feat * width : (feat + 1) * width]
            out_ref[pair * feats + feat, width:] = weight_term[
                top : top + PIECE, left : left + extent
            ]


def backward_kernel(
    table, adj_ref, mine_ref, other_ref, far_ref, same_ref, proj_ref, acc_ref, *tiles
):
    core, side, count = table[0], table[1], table[2]
    row_of, col_of = slots_of(table, adj_ref.shape[0])
    rings = far_ref.shape[0]
    width = acc_ref.shape[1]
    blocks = acc_ref.shape[0] // (rings * SIDES)
    feats = proj_ref.shape[2]
    for pair in range(proj_ref.shape[0]):
        part = slice(pair * feats, (pair + 1) * feats)
        proj_ref[pair, core] = mine_ref[part, :width]
        proj_ref[pair, 1 - core] = other_ref[part, :width]

    def source(slot):
        row = row_of(slot)
        return proj_ref[row // (CORES * feats), (row // feats) % CORES, row % feats]

    accumulate_tiles(count, source, adj_ref, *tiles, acc_ref, col_of, NN)
    weight_term = jnp.sum(mine_ref[:, width:].astype(jnp.float32), axis=0) + jnp.sum(
        other_ref[:, width:].astype(jnp.float32), axis=0
    )
    for ring in range(rings):
        for out_ref, out_side in ((far_ref, 1 - side), (same_ref, side)):
            start = (ring * SIDES + out_side) * blocks
            for block in range(blocks):
                out_ref[ring, block * width : (block + 1) * width] = acc_ref[start + block].astype(
                    out_ref.dtype
                )
        far_ref[ring, blocks * width :] = weight_term.astype(far_ref.dtype)


def reduce_kernel(pieces_ref, grad_ref, weight_ref):
    rows = grad_ref.shape[0]
    grad_ref[...] = jnp.sum(pieces_ref[:, :rows].astype(jnp.float32), axis=0)
    weight_term = jnp.sum(pieces_ref[:, rows:].astype(jnp.float32), axis=0)
    for pair in range(weight_ref.shape[0]):
        weight_ref[pair] = weight_term


def final_kernel(
    scale, same_ref, swapped_ref, near_ref, far_near_ref, grad_ref, weight_ref
):
    width, nodes = grad_ref.shape
    extent = same_ref.shape[2]
    for block in range(nodes // extent):
        part = slice(block * width, (block + 1) * width)
        grad_ref[:, block * extent : (block + 1) * extent] = swapped_ref[part] + jnp.sum(
            same_ref[:, part].astype(jnp.float32), axis=0
        )
    halves = weight_ref.shape[1] // extent
    for pair in range(near_ref.shape[0]):
        top, left = (pair // halves) * PIECE, (pair % halves) * extent
        weight_ref[top : top + PIECE, left : left + extent] = (
            near_ref[pair] + far_near_ref[pair]
        ) * scale


SMEM_SPEC = pl.BlockSpec(memory_space=pltpu.SMEM)
VMEM_SPEC = pl.BlockSpec(memory_space=pltpu.VMEM)


def in_vmem(array):
    return pltpu.with_memory_space_constraint(array, pltpu.VMEM)


def call(kernel, scalars, arrays, out_shapes, scratch=()):
    return pl.pallas_call(
        kernel,
        out_shape=out_shapes,
        in_specs=[SMEM_SPEC] * len(scalars) + [VMEM_SPEC] * len(arrays),
        out_specs=jax.tree.map(lambda _: VMEM_SPEC, out_shapes),
        scratch_shapes=scratch,
        compiler_params=pltpu.CompilerParams(vmem_limit_bytes=VMEM_LIMIT),
    )(*scalars, *(in_vmem(array) for array in arrays))


def tile_call(kernel, scalars, adjacency, arrays, out_shapes, scratch):
    return pl.pallas_call(
        kernel,
        out_shape=out_shapes,
        in_specs=[SMEM_SPEC] * len(scalars)
        + [pl.BlockSpec(memory_space=pltpu.HBM)]
        + [VMEM_SPEC] * len(arrays),
        out_specs=jax.tree.map(lambda _: VMEM_SPEC, out_shapes),
        scratch_shapes=[
            *scratch,
            pltpu.VMEM(adjacency.shape, adjacency.dtype),
            pltpu.SemaphoreType.DMA((adjacency.shape[0] // CHUNK,)),
        ],
        compiler_params=pltpu.CompilerParams(vmem_limit_bytes=VMEM_LIMIT),
    )(
        *scalars,
        pltpu.with_memory_space_constraint(adjacency, pltpu.HBM),
        *(in_vmem(array) for array in arrays),
    )


def local(features, weight, grad_out, adjacency, tile_rows, tile_cols, tile_count):
    nodes, width = features.shape
    extent = adjacency.shape[1]
    rings, near, feats = (lax.axis_size(name) for name in ("ring", "near", "feat"))
    full = feats * width
    blocks = nodes // extent
    owners = near * feats
    swap = [(0, 1), (1, 0)]
    core, side, near_index = (
        lax.axis_index(name).astype(jnp.int32) for name in ("core", "side", "near")
    )
    table = jnp.concatenate([jnp.stack([core, side]), tile_count, tile_rows, tile_cols])
    bf16, f32 = jnp.bfloat16, jnp.float32

    def spread(value):
        copies = call(spread_kernel, (), (value,), pltpu.VMEM((rings, width, nodes), bf16))
        return lax.all_to_all(copies, "ring", 0, 0, tiled=False)

    own = features.T
    partner = lax.ppermute(own, "side", swap)
    same = spread(own)
    same, partner = lax.optimization_barrier((same, partner))
    far = spread(partner)

    half = jax.ShapeDtypeStruct((near, feats, width, extent), f32)
    keep, send = tile_call(
        forward_kernel,
        (table,),
        adjacency,
        (same, far),
        (half, half),
        [pltpu.VMEM((CORES * owners, width, extent), f32)],
    )
    received = lax.ppermute(send, "core", swap)
    flat = (owners, width, extent)
    terms = call(
        combine_kernel,
        (near_index.reshape(1),),
        (keep.reshape(flat), received.reshape(flat), weight),
        pltpu.VMEM((owners, width + PIECE, extent), bf16),
    )
    terms = lax.all_to_all(terms, ("near", "feat"), 0, 0, tiled=False)
    outgoing, activated = call(
        dense_kernel,
        (),
        (terms.reshape(near, feats, width + PIECE, extent), grad_out),
        (
            pltpu.VMEM((owners, width + PIECE, extent), bf16),
            jax.ShapeDtypeStruct((extent, full), bf16),
        ),
        [pltpu.VMEM((full, full), bf16)],
    )

    mine = lax.all_to_all(outgoing, ("near", "feat"), 0, 0, tiled=False)
    other = lax.ppermute(mine, "core", swap)
    far, same = tile_call(
        backward_kernel,
        (table,),
        adjacency,
        (mine, other),
        (
            pltpu.VMEM((rings, blocks * width + PIECE, extent), bf16),
            pltpu.VMEM((rings, blocks * width, extent), bf16),
        ),
        [
            pltpu.VMEM((near, CORES, feats, width, extent), bf16),
            pltpu.VMEM((rings * SIDES * blocks, width, extent), f32),
        ],
    )
    far = lax.all_to_all(far, "ring", 0, 0, tiled=False)
    summed, weight_piece = call(
        reduce_kernel,
        (),
        (far,),
        (
            jax.ShapeDtypeStruct((blocks * width, extent), f32),
            pltpu.VMEM((near, PIECE, extent), f32),
        ),
    )
    swapped = lax.ppermute(summed, "side", swap)
    same, weight_piece = lax.optimization_barrier((same, weight_piece))
    same = lax.all_to_all(same, "ring", 0, 0, tiled=False)
    weight_piece = lax.all_to_all(weight_piece, "near", 0, 0, tiled=False)
    far_weight_piece = lax.ppermute(weight_piece, "side", swap)
    scale = 1.0 / math.sqrt(nodes * rings * SIDES * near * CORES)
    feature_grad, weight_grad = call(
        lambda *refs: final_kernel(scale, *refs),
        (),
        (same, swapped, weight_piece, far_weight_piece),
        (
            jax.ShapeDtypeStruct((width, nodes), f32),
            jax.ShapeDtypeStruct((width, full), f32),
        ),
    )
    return (activated, weight_grad, feature_grad.T)


def solution(mesh):
    rows, cols, feats = (mesh.shape[name] for name in ("row", "col", "feat"))
    fine = jax.sharding.Mesh(
        mesh.devices.reshape(rows // SIDES, SIDES, cols // CORES, CORES, feats),
        ("ring", "side", "near", "core", "feat"),
    )
    pair = P(("ring", "side", "near", "core"))
    owner = P(("ring", "side", "near", "core", "feat"), None)
    by_column = P(("near", "core", "ring", "side"), "feat")
    return jax.shard_map(
        local,
        mesh=fine,
        in_specs=(by_column, P("feat", None), owner, pair, pair, pair, pair),
        out_specs=(owner, P("feat", None), by_column),
        check_vma=False,
    )
```

```python
import math

import jax
import jax.numpy as jnp
from jax import lax
from jax.experimental import pallas as pl
from jax.experimental.pallas import tpu as pltpu
from jax.sharding import PartitionSpec as P

CHUNK = 32
PIECE = 16
CORES = 2
SIDES = 2
HEAD = 3
VMEM_LIMIT = 24 * 1024 * 1024
NT = (((1,), (1,)), ((), ()))
NN = (((1,), (0,)), ((), ()))
TN = (((0,), (0,)), ((), ()))


def dot(a, b, dims):
    return lax.dot_general(a, b, dims, preferred_element_type=jnp.float32)


def accumulate_tiles(count, source, adj_ref, tiles_ref, done, acc_ref, target_of, dims):
    chunks, extent = adj_ref.shape[0] // CHUNK, adj_ref.shape[1]

    def load(chunk):
        part = pl.ds(chunk * CHUNK, CHUNK)
        return pltpu.make_async_copy(adj_ref.at[part], tiles_ref.at[part], done.at[chunk])

    for chunk in range(chunks):
        load(chunk).start()
    acc_ref[...] = jnp.zeros_like(acc_ref)

    def product(slot):
        one, two = source(slot), source(slot + 1)
        zero = jnp.zeros_like(one)
        left = jnp.concatenate(
            [jnp.concatenate([one, zero], axis=1), jnp.concatenate([zero, two], axis=1)], axis=0
        )
        if dims is NN:
            right = tiles_ref[pl.ds(slot, 2)].reshape(2 * extent, extent)
        else:
            right = jnp.concatenate([tiles_ref[slot], tiles_ref[slot + 1]], axis=1)
        both = dot(left, right, dims)
        return both[: one.shape[0]], both[one.shape[0] :]

    @pl.loop(0, chunks)
    def _(chunk):
        load(chunk).wait()
        first = chunk * CHUNK

        @pl.when(first < count)
        def _():
            terms = [term for u in range(0, CHUNK, 2) for term in product(first + u)]
            for u, term in enumerate(terms):
                target = target_of(first + u)
                acc_ref[target] += jnp.where(first + u < count, term, 0.0)


def slots_of(table, slots):
    return lambda s: table[HEAD + s], lambda s: table[HEAD + slots + s]


def forward_kernel(table, adj_ref, same_ref, far_ref, keep_ref, send_ref, acc_ref, *tiles):
    core, side, count = table[0], table[1], table[2]
    slots, extent, _ = adj_ref.shape
    blocks = same_ref.shape[2] // extent
    row_of, col_of = slots_of(table, slots)

    def source(slot):
        col = col_of(slot)
        row_device = col // blocks
        nodes = pl.ds(pl.multiple_of((col % blocks) * extent, extent), extent)
        ring = row_device // SIDES
        return jnp.where(
            row_device % SIDES == side, same_ref[ring, :, nodes], far_ref[ring, :, nodes]
        )

    accumulate_tiles(count, source, adj_ref, *tiles, acc_ref, row_of, NT)
    near, feats = keep_ref.shape[:2]
    for pair in range(near):
        keep_ref[pair] = acc_ref[pl.ds((pair * CORES + core) * feats, feats)]
        send_ref[pair] = acc_ref[pl.ds((pair * CORES + 1 - core) * feats, feats)]


def spread_kernel(value_ref, out_ref):
    for copy in range(out_ref.shape[0]):
        out_ref[copy] = value_ref[...]


def combine_kernel(near, keep_ref, received_ref, weight_ref, out_ref):
    owners, width, extent = keep_ref.shape
    halves = weight_ref.shape[1] // extent
    out_ref[:, :width] = (keep_ref[...] + received_ref[...]).astype(out_ref.dtype)
    top = pl.multiple_of((near[0] // halves) * PIECE, PIECE)
    left = pl.multiple_of((near[0] % halves) * extent, extent)
    piece = weight_ref[pl.ds(top, PIECE), pl.ds(left, extent)]
    for owner in range(owners):
        out_ref[owner, width:] = piece


def dense_kernel(terms_ref, grad_ref, out_ref, act_ref, weight_ref):
    near, feats, height, extent = terms_ref.shape
    width = height - PIECE
    full = feats * width
    halves = full // extent
    for pair in range(near):
        for feat in range(feats):
            top = feat * width + (pair // halves) * PIECE
            left = (pair % halves) * extent
            weight_ref[top : top + PIECE, left : left + extent] = terms_ref[pair, feat, width:]
    weight = weight_ref[...]
    summed = jnp.sum(terms_ref[:, :, :width].astype(jnp.float32), axis=0).reshape(full, extent)
    high = summed.astype(jnp.bfloat16)
    low = (summed - high.astype(jnp.float32)).astype(jnp.bfloat16)
    pre_act = dot(high, weight, TN) + dot(low, weight, TN)
    gate = jax.nn.sigmoid(pre_act)
    act_ref[...] = (pre_act * gate).astype(act_ref.dtype)
    derivative = gate * (1.0 + pre_act * (1.0 - gate))
    grad_pre = (grad_ref[...].astype(jnp.float32) * derivative).astype(jnp.bfloat16)
    projected = dot(weight, grad_pre, NT).astype(out_ref.dtype)
    weight_term = (dot(high, grad_pre, NN) + dot(low, grad_pre, NN)).astype(out_ref.dtype)
    for pair in range(near):
        for feat in range(feats):
            top = feat * width + (pair // halves) * PIECE
            left = (pair % halves) * extent
            out_ref[pair * feats + feat, :width] = projected[feat * width : (feat + 1) * width]
            out_ref[pair * feats + feat, width:] = weight_term[
                top : top + PIECE, left : left + extent
            ]


def backward_kernel(
    table, adj_ref, mine_ref, other_ref, out_ref, proj_ref, acc_ref, *tiles
):
    core, count = table[0], table[2]
    row_of, col_of = slots_of(table, adj_ref.shape[0])
    rows = out_ref.shape[0]
    width = acc_ref.shape[1]
    blocks = acc_ref.shape[0] // rows
    feats = proj_ref.shape[2]
    for pair in range(proj_ref.shape[0]):
        part = slice(pair * feats, (pair + 1) * feats)
        proj_ref[pair, core] = mine_ref[part, :width]
        proj_ref[pair, 1 - core] = other_ref[part, :width]

    def source(slot):
        row = row_of(slot)
        return proj_ref[row // (CORES * feats), (row // feats) % CORES, row % feats]

    accumulate_tiles(count, source, adj_ref, *tiles, acc_ref, col_of, NN)
    weight_term = jnp.sum(mine_ref[:, width:].astype(jnp.float32), axis=0) + jnp.sum(
        other_ref[:, width:].astype(jnp.float32), axis=0
    )
    for row in range(rows):
        for block in range(blocks):
            out_ref[row, block * width : (block + 1) * width] = acc_ref[
                row * blocks + block
            ].astype(out_ref.dtype)
        out_ref[row, blocks * width :] = weight_term.astype(out_ref.dtype)


def final_kernel(scale, pieces_ref, grad_ref, weight_ref):
    width, nodes = grad_ref.shape
    extent = pieces_ref.shape[2]
    for block in range(nodes // extent):
        grad_ref[:, block * extent : (block + 1) * extent] = jnp.sum(
            pieces_ref[:, block * width : (block + 1) * width].astype(jnp.float32), axis=0
        )
    rest = pieces_ref[:, nodes // extent * width :].astype(jnp.float32)
    weight_term = jnp.sum(rest, axis=0) * scale
    for pair in range(weight_ref.shape[0]):
        weight_ref[pair] = weight_term


SMEM_SPEC = pl.BlockSpec(memory_space=pltpu.SMEM)
VMEM_SPEC = pl.BlockSpec(memory_space=pltpu.VMEM)


def in_vmem(array):
    return pltpu.with_memory_space_constraint(array, pltpu.VMEM)


def call(kernel, scalars, arrays, out_shapes, scratch=()):
    return pl.pallas_call(
        kernel,
        out_shape=out_shapes,
        in_specs=[SMEM_SPEC] * len(scalars) + [VMEM_SPEC] * len(arrays),
        out_specs=jax.tree.map(lambda _: VMEM_SPEC, out_shapes),
        scratch_shapes=scratch,
        compiler_params=pltpu.CompilerParams(vmem_limit_bytes=VMEM_LIMIT),
    )(*scalars, *(in_vmem(array) for array in arrays))


def tile_call(kernel, scalars, adjacency, arrays, out_shapes, scratch):
    return pl.pallas_call(
        kernel,
        out_shape=out_shapes,
        in_specs=[SMEM_SPEC] * len(scalars)
        + [pl.BlockSpec(memory_space=pltpu.HBM)]
        + [VMEM_SPEC] * len(arrays),
        out_specs=jax.tree.map(lambda _: VMEM_SPEC, out_shapes),
        scratch_shapes=[
            *scratch,
            pltpu.VMEM(adjacency.shape, adjacency.dtype),
            pltpu.SemaphoreType.DMA((adjacency.shape[0] // CHUNK,)),
        ],
        compiler_params=pltpu.CompilerParams(vmem_limit_bytes=VMEM_LIMIT),
    )(
        *scalars,
        pltpu.with_memory_space_constraint(adjacency, pltpu.HBM),
        *(in_vmem(array) for array in arrays),
    )


def local(features, weight, grad_out, adjacency, tile_rows, tile_cols, tile_count):
    nodes, width = features.shape
    extent = adjacency.shape[1]
    rings, near, feats = (lax.axis_size(name) for name in ("ring", "near", "feat"))
    full = feats * width
    blocks = nodes // extent
    owners = near * feats
    swap = [(0, 1), (1, 0)]
    core, side, near_index = (
        lax.axis_index(name).astype(jnp.int32) for name in ("core", "side", "near")
    )
    table = jnp.concatenate([jnp.stack([core, side]), tile_count, tile_rows, tile_cols])
    bf16, f32 = jnp.bfloat16, jnp.float32

    def spread(value):
        copies = call(spread_kernel, (), (value,), pltpu.VMEM((rings, width, nodes), bf16))
        return lax.all_to_all(copies, "ring", 0, 0, tiled=False)

    own = features.T
    partner = lax.ppermute(own, "side", swap)
    same = spread(own)
    same, partner = lax.optimization_barrier((same, partner))
    far = spread(partner)

    half = jax.ShapeDtypeStruct((near, feats, width, extent), f32)
    keep, send = tile_call(
        forward_kernel,
        (table,),
        adjacency,
        (same, far),
        (half, half),
        [pltpu.VMEM((CORES * owners, width, extent), f32)],
    )
    received = lax.ppermute(send, "core", swap)
    flat = (owners, width, extent)
    terms = call(
        combine_kernel,
        (near_index.reshape(1),),
        (keep.reshape(flat), received.reshape(flat), weight),
        pltpu.VMEM((owners, width + PIECE, extent), bf16),
    )
    terms = lax.all_to_all(terms, ("near", "feat"), 0, 0, tiled=False)
    outgoing, activated = call(
        dense_kernel,
        (),
        (terms.reshape(near, feats, width + PIECE, extent), grad_out),
        (
            pltpu.VMEM((owners, width + PIECE, extent), bf16),
            jax.ShapeDtypeStruct((extent, full), bf16),
        ),
        [pltpu.VMEM((full, full), bf16)],
    )

    mine = lax.all_to_all(outgoing, ("near", "feat"), 0, 0, tiled=False)
    other = lax.ppermute(mine, "core", swap)
    pieces = tile_call(
        backward_kernel,
        (table,),
        adjacency,
        (mine, other),
        pltpu.VMEM((rings * SIDES, blocks * width + PIECE, extent), bf16),
        [
            pltpu.VMEM((near, CORES, feats, width, extent), bf16),
            pltpu.VMEM((rings * SIDES * blocks, width, extent), f32),
        ],
    )
    pieces = lax.all_to_all(pieces, ("ring", "side"), 0, 0, tiled=False)
    scale = 1.0 / math.sqrt(nodes * rings * SIDES * near * CORES)
    feature_grad, weight_piece = call(
        lambda *refs: final_kernel(scale, *refs),
        (),
        (pieces,),
        (
            jax.ShapeDtypeStruct((width, nodes), f32),
            pltpu.VMEM((near, PIECE, extent), f32),
        ),
    )
    weight_grad = lax.all_to_all(weight_piece, "near", 0, 0, tiled=False)
    weight_grad = weight_grad.reshape(width // PIECE, full // extent, PIECE, extent)
    weight_grad = weight_grad.transpose(0, 2, 1, 3).reshape(width, full)
    return (activated, weight_grad, feature_grad.T)


def solution(mesh):
    rows, cols, feats = (mesh.shape[name] for name in ("row", "col", "feat"))
    fine = jax.sharding.Mesh(
        mesh.devices.reshape(rows // SIDES, SIDES, cols // CORES, CORES, feats),
        ("ring", "side", "near", "core", "feat"),
    )
    pair = P(("ring", "side", "near", "core"))
    owner = P(("ring", "side", "near", "core", "feat"), None)
    by_column = P(("near", "core", "ring", "side"), "feat")
    return jax.shard_map(
        local,
        mesh=fine,
        in_specs=(by_column, P("feat", None), owner, pair, pair, pair, pair),
        out_specs=(owner, P("feat", None), by_column),
        check_vma=False,
    )
```

```python
import math

import jax
import jax.numpy as jnp
from jax import lax
from jax.experimental import pallas as pl
from jax.experimental.pallas import tpu as pltpu
from jax.sharding import PartitionSpec as P

CHUNK = 32
PIECE = 16
CORES = 2
SIDES = 2
HEAD = 3
VMEM_LIMIT = 24 * 1024 * 1024
NT = (((1,), (1,)), ((), ()))
NN = (((1,), (0,)), ((), ()))
TN = (((0,), (0,)), ((), ()))


def dot(a, b, dims):
    return lax.dot_general(a, b, dims, preferred_element_type=jnp.float32)


def accumulate_tiles(count, source, adj_ref, tiles_ref, done, acc_ref, target_of, dims):
    chunks, extent = adj_ref.shape[0] // CHUNK, adj_ref.shape[1]

    def load(chunk):
        part = pl.ds(chunk * CHUNK, CHUNK)
        return pltpu.make_async_copy(adj_ref.at[part], tiles_ref.at[part], done.at[chunk])

    for chunk in range(chunks):
        load(chunk).start()
    acc_ref[...] = jnp.zeros_like(acc_ref)

    def product(slot):
        one, two = source(slot), source(slot + 1)
        zero = jnp.zeros_like(one)
        left = jnp.concatenate(
            [jnp.concatenate([one, zero], axis=1), jnp.concatenate([zero, two], axis=1)], axis=0
        )
        if dims is NN:
            right = tiles_ref[pl.ds(slot, 2)].reshape(2 * extent, extent)
        else:
            right = jnp.concatenate([tiles_ref[slot], tiles_ref[slot + 1]], axis=1)
        both = dot(left, right, dims)
        return both[: one.shape[0]], both[one.shape[0] :]

    @pl.loop(0, chunks)
    def _(chunk):
        load(chunk).wait()
        first = chunk * CHUNK

        @pl.when(first < count)
        def _():
            terms = [term for u in range(0, CHUNK, 2) for term in product(first + u)]
            for u, term in enumerate(terms):
                target = target_of(first + u)
                acc_ref[target] += jnp.where(first + u < count, term, 0.0)


def slots_of(table, slots):
    return lambda s: table[HEAD + s], lambda s: table[HEAD + slots + s]


def forward_kernel(table, adj_ref, same_ref, far_ref, keep_ref, send_ref, acc_ref, *tiles):
    core, side, count = table[0], table[1], table[2]
    slots, extent, _ = adj_ref.shape
    blocks = same_ref.shape[2] // extent
    row_of, col_of = slots_of(table, slots)

    def source(slot):
        col = col_of(slot)
        row_device = col // blocks
        nodes = pl.ds(pl.multiple_of((col % blocks) * extent, extent), extent)
        ring = row_device // SIDES
        return jnp.where(
            row_device % SIDES == side, same_ref[ring, :, nodes], far_ref[ring, :, nodes]
        )

    accumulate_tiles(count, source, adj_ref, *tiles, acc_ref, row_of, NT)
    near, feats = keep_ref.shape[:2]
    for pair in range(near):
        keep_ref[pair] = acc_ref[pl.ds((pair * CORES + core) * feats, feats)]
        send_ref[pair] = acc_ref[pl.ds((pair * CORES + 1 - core) * feats, feats)]


def spread_kernel(value_ref, out_ref):
    for copy in range(out_ref.shape[0]):
        out_ref[copy] = value_ref[...]


def combine_kernel(near, keep_ref, received_ref, weight_ref, out_ref):
    owners, width, extent = keep_ref.shape
    halves = weight_ref.shape[1] // extent
    out_ref[:, :width] = (keep_ref[...] + received_ref[...]).astype(out_ref.dtype)
    top = pl.multiple_of((near[0] // halves) * PIECE, PIECE)
    left = pl.multiple_of((near[0] % halves) * extent, extent)
    piece = weight_ref[pl.ds(top, PIECE), pl.ds(left, extent)]
    for owner in range(owners):
        out_ref[owner, width:] = piece


def dense_kernel(terms_ref, grad_ref, out_ref, act_ref, weight_ref):
    near, feats, height, extent = terms_ref.shape
    width = height - PIECE
    full = feats * width
    halves = full // extent
    for pair in range(near):
        for feat in range(feats):
            top = feat * width + (pair // halves) * PIECE
            left = (pair % halves) * extent
            weight_ref[top : top + PIECE, left : left + extent] = terms_ref[pair, feat, width:]
    weight = weight_ref[...]
    summed = jnp.sum(terms_ref[:, :, :width].astype(jnp.float32), axis=0).reshape(full, extent)
    high = summed.astype(jnp.bfloat16)
    low = (summed - high.astype(jnp.float32)).astype(jnp.bfloat16)
    pre_act = dot(high, weight, TN) + dot(low, weight, TN)
    gate = jax.nn.sigmoid(pre_act)
    act_ref[...] = (pre_act * gate).astype(act_ref.dtype)
    derivative = gate * (1.0 + pre_act * (1.0 - gate))
    grad_pre = (grad_ref[...].astype(jnp.float32) * derivative).astype(jnp.bfloat16)
    projected = dot(weight, grad_pre, NT).astype(out_ref.dtype)
    weight_term = (dot(high, grad_pre, NN) + dot(low, grad_pre, NN)).astype(out_ref.dtype)
    for pair in range(near):
        for feat in range(feats):
            top = feat * width + (pair // halves) * PIECE
            left = (pair % halves) * extent
            out_ref[pair * feats + feat, :width] = projected[feat * width : (feat + 1) * width]
            out_ref[pair * feats + feat, width:] = weight_term[
                top : top + PIECE, left : left + extent
            ]


def backward_kernel(
    table, adj_ref, mine_ref, other_ref, out_ref, proj_ref, acc_ref, *tiles
):
    core, side, count = table[0], table[1], table[2]
    row_of, col_of = slots_of(table, adj_ref.shape[0])
    rings = out_ref.shape[0]
    width = acc_ref.shape[1]
    blocks = acc_ref.shape[0] // (rings * SIDES)
    feats = proj_ref.shape[2]
    for pair in range(proj_ref.shape[0]):
        part = slice(pair * feats, (pair + 1) * feats)
        proj_ref[pair, core] = mine_ref[part, :width]
        proj_ref[pair, 1 - core] = other_ref[part, :width]

    def source(slot):
        row = row_of(slot)
        return proj_ref[row // (CORES * feats), (row // feats) % CORES, row % feats]

    accumulate_tiles(count, source, adj_ref, *tiles, acc_ref, col_of, NN)
    weight_term = jnp.sum(mine_ref[:, width:].astype(jnp.float32), axis=0) + jnp.sum(
        other_ref[:, width:].astype(jnp.float32), axis=0
    )
    for ring in range(rings):
        for part, out_side in enumerate((1 - side, side)):
            start = (ring * SIDES + out_side) * blocks
            for block in range(blocks):
                top = (part * blocks + block) * width
                out_ref[ring, top : top + width] = acc_ref[start + block].astype(out_ref.dtype)
        out_ref[ring, SIDES * blocks * width :] = weight_term.astype(out_ref.dtype)


def reduce_kernel(pieces_ref, far_ref, same_ref, weight_ref):
    rows = far_ref.shape[0]
    far_ref[...] = jnp.sum(pieces_ref[:, :rows].astype(jnp.float32), axis=0)
    same_ref[...] = jnp.sum(pieces_ref[:, rows : 2 * rows].astype(jnp.float32), axis=0)
    weight_term = jnp.sum(pieces_ref[:, 2 * rows :].astype(jnp.float32), axis=0)
    for copy in range(weight_ref.shape[0]):
        weight_ref[copy] = weight_term


def final_kernel(scale, same_ref, swapped_ref, terms_ref, grad_ref, weight_ref):
    width, nodes = grad_ref.shape
    extent = same_ref.shape[1]
    for block in range(nodes // extent):
        part = slice(block * width, (block + 1) * width)
        grad_ref[:, block * extent : (block + 1) * extent] = same_ref[part] + swapped_ref[part]
    halves = weight_ref.shape[1] // extent
    near = terms_ref.shape[0] // SIDES
    for pair in range(near):
        top, left = (pair // halves) * PIECE, (pair % halves) * extent
        weight_ref[top : top + PIECE, left : left + extent] = (
            terms_ref[pair] + terms_ref[near + pair]
        ) * scale


SMEM_SPEC = pl.BlockSpec(memory_space=pltpu.SMEM)
VMEM_SPEC = pl.BlockSpec(memory_space=pltpu.VMEM)


def in_vmem(array):
    return pltpu.with_memory_space_constraint(array, pltpu.VMEM)


def call(kernel, scalars, arrays, out_shapes, scratch=()):
    return pl.pallas_call(
        kernel,
        out_shape=out_shapes,
        in_specs=[SMEM_SPEC] * len(scalars) + [VMEM_SPEC] * len(arrays),
        out_specs=jax.tree.map(lambda _: VMEM_SPEC, out_shapes),
        scratch_shapes=scratch,
        compiler_params=pltpu.CompilerParams(vmem_limit_bytes=VMEM_LIMIT),
    )(*scalars, *(in_vmem(array) for array in arrays))


def tile_call(kernel, scalars, adjacency, arrays, out_shapes, scratch):
    return pl.pallas_call(
        kernel,
        out_shape=out_shapes,
        in_specs=[SMEM_SPEC] * len(scalars)
        + [pl.BlockSpec(memory_space=pltpu.HBM)]
        + [VMEM_SPEC] * len(arrays),
        out_specs=jax.tree.map(lambda _: VMEM_SPEC, out_shapes),
        scratch_shapes=[
            *scratch,
            pltpu.VMEM(adjacency.shape, adjacency.dtype),
            pltpu.SemaphoreType.DMA((adjacency.shape[0] // CHUNK,)),
        ],
        compiler_params=pltpu.CompilerParams(vmem_limit_bytes=VMEM_LIMIT),
    )(
        *scalars,
        pltpu.with_memory_space_constraint(adjacency, pltpu.HBM),
        *(in_vmem(array) for array in arrays),
    )


def local(features, weight, grad_out, adjacency, tile_rows, tile_cols, tile_count):
    nodes, width = features.shape
    extent = adjacency.shape[1]
    rings, near, feats = (lax.axis_size(name) for name in ("ring", "near", "feat"))
    full = feats * width
    blocks = nodes // extent
    owners = near * feats
    swap = [(0, 1), (1, 0)]
    core, side, near_index = (
        lax.axis_index(name).astype(jnp.int32) for name in ("core", "side", "near")
    )
    table = jnp.concatenate([jnp.stack([core, side]), tile_count, tile_rows, tile_cols])
    bf16, f32 = jnp.bfloat16, jnp.float32

    def spread(value):
        copies = call(spread_kernel, (), (value,), pltpu.VMEM((rings, width, nodes), bf16))
        return lax.all_to_all(copies, "ring", 0, 0, tiled=False)

    own = features.T
    partner = lax.ppermute(own, "side", swap)
    same = spread(own)
    same, partner = lax.optimization_barrier((same, partner))
    far = spread(partner)

    half = jax.ShapeDtypeStruct((near, feats, width, extent), f32)
    keep, send = tile_call(
        forward_kernel,
        (table,),
        adjacency,
        (same, far),
        (half, half),
        [pltpu.VMEM((CORES * owners, width, extent), f32)],
    )
    received = lax.ppermute(send, "core", swap)
    flat = (owners, width, extent)
    terms = call(
        combine_kernel,
        (near_index.reshape(1),),
        (keep.reshape(flat), received.reshape(flat), weight),
        pltpu.VMEM((owners, width + PIECE, extent), bf16),
    )
    terms = lax.all_to_all(terms, ("near", "feat"), 0, 0, tiled=False)
    outgoing, activated = call(
        dense_kernel,
        (),
        (terms.reshape(near, feats, width + PIECE, extent), grad_out),
        (
            pltpu.VMEM((owners, width + PIECE, extent), bf16),
            jax.ShapeDtypeStruct((extent, full), bf16),
        ),
        [pltpu.VMEM((full, full), bf16)],
    )

    mine = lax.all_to_all(outgoing, ("near", "feat"), 0, 0, tiled=False)
    other = lax.ppermute(mine, "core", swap)
    pieces = tile_call(
        backward_kernel,
        (table,),
        adjacency,
        (mine, other),
        pltpu.VMEM((rings, SIDES * blocks * width + PIECE, extent), bf16),
        [
            pltpu.VMEM((near, CORES, feats, width, extent), bf16),
            pltpu.VMEM((rings * SIDES * blocks, width, extent), f32),
        ],
    )
    pieces = lax.all_to_all(pieces, "ring", 0, 0, tiled=False)
    block_sum = jax.ShapeDtypeStruct((blocks * width, extent), f32)
    other_side, this_side, weight_piece = call(
        reduce_kernel,
        (),
        (pieces,),
        (block_sum, block_sum, pltpu.VMEM((SIDES * near, PIECE, extent), f32)),
    )
    swapped = lax.ppermute(other_side, "side", swap)
    weight_terms = lax.all_to_all(weight_piece, ("side", "near"), 0, 0, tiled=False)
    scale = 1.0 / math.sqrt(nodes * rings * SIDES * near * CORES)
    feature_grad, weight_grad = call(
        lambda *refs: final_kernel(scale, *refs),
        (),
        (this_side, swapped, weight_terms),
        (
            jax.ShapeDtypeStruct((width, nodes), f32),
            jax.ShapeDtypeStruct((width, full), f32),
        ),
    )
    return (activated, weight_grad, feature_grad.T)


def solution(mesh):
    rows, cols, feats = (mesh.shape[name] for name in ("row", "col", "feat"))
    fine = jax.sharding.Mesh(
        mesh.devices.reshape(rows // SIDES, SIDES, cols // CORES, CORES, feats),
        ("ring", "side", "near", "core", "feat"),
    )
    pair = P(("ring", "side", "near", "core"))
    owner = P(("ring", "side", "near", "core", "feat"), None)
    by_column = P(("near", "core", "ring", "side"), "feat")
    return jax.shard_map(
        local,
        mesh=fine,
        in_specs=(by_column, P("feat", None), owner, pair, pair, pair, pair),
        out_specs=(owner, P("feat", None), by_column),
        check_vma=False,
    )
```

```python
import math

import jax
import jax.numpy as jnp
from jax import lax
from jax.experimental import pallas as pl
from jax.experimental.pallas import tpu as pltpu
from jax.sharding import PartitionSpec as P

CHUNK = 32
PIECE = 16
CORES = 2
SIDES = 2
HEAD = 3
VMEM_LIMIT = 24 * 1024 * 1024
NT = (((1,), (1,)), ((), ()))
NN = (((1,), (0,)), ((), ()))
TN = (((0,), (0,)), ((), ()))


def dot(a, b, dims):
    return lax.dot_general(a, b, dims, preferred_element_type=jnp.float32)


def accumulate_tiles(count, source, adj_ref, tiles_ref, done, acc_ref, target_of, dims):
    chunks, extent = adj_ref.shape[0] // CHUNK, adj_ref.shape[1]

    def load(chunk):
        part = pl.ds(chunk * CHUNK, CHUNK)
        return pltpu.make_async_copy(adj_ref.at[part], tiles_ref.at[part], done.at[chunk])

    for chunk in range(chunks):
        load(chunk).start()
    acc_ref[...] = jnp.zeros_like(acc_ref)

    def product(slot):
        one, two = source(slot), source(slot + 1)
        zero = jnp.zeros_like(one)
        left = jnp.concatenate(
            [jnp.concatenate([one, zero], axis=1), jnp.concatenate([zero, two], axis=1)], axis=0
        )
        if dims is NN:
            right = tiles_ref[pl.ds(slot, 2)].reshape(2 * extent, extent)
        else:
            right = jnp.concatenate([tiles_ref[slot], tiles_ref[slot + 1]], axis=1)
        both = dot(left, right, dims)
        return both[: one.shape[0]], both[one.shape[0] :]

    @pl.loop(0, chunks)
    def _(chunk):
        load(chunk).wait()
        first = chunk * CHUNK

        @pl.when(first < count)
        def _():
            terms = [term for u in range(0, CHUNK, 2) for term in product(first + u)]
            for u, term in enumerate(terms):
                target = target_of(first + u)
                acc_ref[target] += jnp.where(first + u < count, term, 0.0)


def slots_of(table, slots):
    return lambda s: table[HEAD + s], lambda s: table[HEAD + slots + s]


def forward_kernel(table, adj_ref, same_ref, far_ref, keep_ref, send_ref, acc_ref, *tiles):
    core, side, count = table[0], table[1], table[2]
    slots, extent, _ = adj_ref.shape
    blocks = same_ref.shape[2] // extent
    row_of, col_of = slots_of(table, slots)

    def source(slot):
        col = col_of(slot)
        row_device = col // blocks
        nodes = pl.ds(pl.multiple_of((col % blocks) * extent, extent), extent)
        ring = row_device // SIDES
        return jnp.where(
            row_device % SIDES == side, same_ref[ring, :, nodes], far_ref[ring, :, nodes]
        )

    accumulate_tiles(count, source, adj_ref, *tiles, acc_ref, row_of, NT)
    near, feats = keep_ref.shape[:2]
    for pair in range(near):
        keep_ref[pair] = acc_ref[pl.ds((pair * CORES + core) * feats, feats)]
        send_ref[pair] = acc_ref[pl.ds((pair * CORES + 1 - core) * feats, feats)]


def spread_kernel(value_ref, out_ref):
    for copy in range(out_ref.shape[0]):
        out_ref[copy] = value_ref[...]


def combine_kernel(near, keep_ref, received_ref, weight_ref, out_ref):
    owners, width, extent = keep_ref.shape
    halves = weight_ref.shape[1] // extent
    out_ref[:, :width] = (keep_ref[...] + received_ref[...]).astype(out_ref.dtype)
    top = pl.multiple_of((near[0] // halves) * PIECE, PIECE)
    left = pl.multiple_of((near[0] % halves) * extent, extent)
    piece = weight_ref[pl.ds(top, PIECE), pl.ds(left, extent)]
    for owner in range(owners):
        out_ref[owner, width:] = piece


def dense_kernel(terms_ref, grad_ref, out_ref, act_ref, weight_ref):
    near, feats, height, extent = terms_ref.shape
    width = height - PIECE
    full = feats * width
    halves = full // extent
    for pair in range(near):
        for feat in range(feats):
            top = feat * width + (pair // halves) * PIECE
            left = (pair % halves) * extent
            weight_ref[top : top + PIECE, left : left + extent] = terms_ref[pair, feat, width:]
    weight = weight_ref[...]
    summed = jnp.sum(terms_ref[:, :, :width].astype(jnp.float32), axis=0).reshape(full, extent)
    high = summed.astype(jnp.bfloat16)
    low = (summed - high.astype(jnp.float32)).astype(jnp.bfloat16)
    pre_act = dot(high, weight, TN) + dot(low, weight, TN)
    gate = jax.nn.sigmoid(pre_act)
    act_ref[...] = (pre_act * gate).astype(act_ref.dtype)
    derivative = gate * (1.0 + pre_act * (1.0 - gate))
    grad_pre = (grad_ref[...].astype(jnp.float32) * derivative).astype(jnp.bfloat16)
    projected = dot(weight, grad_pre, NT).astype(out_ref.dtype)
    weight_term = (dot(high, grad_pre, NN) + dot(low, grad_pre, NN)).astype(out_ref.dtype)
    for pair in range(near):
        for feat in range(feats):
            top = feat * width + (pair // halves) * PIECE
            left = (pair % halves) * extent
            out_ref[pair * feats + feat, :width] = projected[feat * width : (feat + 1) * width]
            out_ref[pair * feats + feat, width:] = weight_term[
                top : top + PIECE, left : left + extent
            ]


def backward_kernel(
    table, adj_ref, mine_ref, other_ref, out_ref, proj_ref, acc_ref, *tiles
):
    core, side, count = table[0], table[1], table[2]
    row_of, col_of = slots_of(table, adj_ref.shape[0])
    rings = out_ref.shape[0]
    width = acc_ref.shape[1]
    blocks = acc_ref.shape[0] // (rings * SIDES)
    feats = proj_ref.shape[2]
    for pair in range(proj_ref.shape[0]):
        part = slice(pair * feats, (pair + 1) * feats)
        proj_ref[pair, core] = mine_ref[part, :width]
        proj_ref[pair, 1 - core] = other_ref[part, :width]

    def source(slot):
        row = row_of(slot)
        return proj_ref[row // (CORES * feats), (row // feats) % CORES, row % feats]

    accumulate_tiles(count, source, adj_ref, *tiles, acc_ref, col_of, NN)
    weight_term = jnp.sum(mine_ref[:, width:].astype(jnp.float32), axis=0) + jnp.sum(
        other_ref[:, width:].astype(jnp.float32), axis=0
    )
    for ring in range(rings):
        for part, out_side in enumerate((1 - side, side)):
            start = (ring * SIDES + out_side) * blocks
            for block in range(blocks):
                top = (part * blocks + block) * width
                out_ref[ring, top : top + width] = acc_ref[start + block].astype(out_ref.dtype)
        out_ref[ring, SIDES * blocks * width :] = weight_term.astype(out_ref.dtype)


def reduce_kernel(pieces_ref, far_ref, same_ref, weight_ref):
    rows = far_ref.shape[0]
    far_ref[...] = jnp.sum(pieces_ref[:, :rows].astype(jnp.float32), axis=0).astype(far_ref.dtype)
    same_ref[...] = jnp.sum(pieces_ref[:, rows : 2 * rows].astype(jnp.float32), axis=0)
    weight_term = jnp.sum(pieces_ref[:, 2 * rows :].astype(jnp.float32), axis=0)
    for copy in range(weight_ref.shape[0]):
        weight_ref[copy] = weight_term


def final_kernel(scale, same_ref, swapped_ref, terms_ref, grad_ref, weight_ref):
    width, nodes = grad_ref.shape
    extent = same_ref.shape[1]
    for block in range(nodes // extent):
        part = slice(block * width, (block + 1) * width)
        grad_ref[:, block * extent : (block + 1) * extent] = same_ref[part] + swapped_ref[
            part
        ].astype(jnp.float32)
    halves = weight_ref.shape[1] // extent
    near = terms_ref.shape[0] // SIDES
    for pair in range(near):
        top, left = (pair // halves) * PIECE, (pair % halves) * extent
        weight_ref[top : top + PIECE, left : left + extent] = (
            terms_ref[pair] + terms_ref[near + pair]
        ) * scale


SMEM_SPEC = pl.BlockSpec(memory_space=pltpu.SMEM)
VMEM_SPEC = pl.BlockSpec(memory_space=pltpu.VMEM)


def in_vmem(array):
    return pltpu.with_memory_space_constraint(array, pltpu.VMEM)


def call(kernel, scalars, arrays, out_shapes, scratch=()):
    return pl.pallas_call(
        kernel,
        out_shape=out_shapes,
        in_specs=[SMEM_SPEC] * len(scalars) + [VMEM_SPEC] * len(arrays),
        out_specs=jax.tree.map(lambda _: VMEM_SPEC, out_shapes),
        scratch_shapes=scratch,
        compiler_params=pltpu.CompilerParams(vmem_limit_bytes=VMEM_LIMIT),
    )(*scalars, *(in_vmem(array) for array in arrays))


def tile_call(kernel, scalars, adjacency, arrays, out_shapes, scratch):
    return pl.pallas_call(
        kernel,
        out_shape=out_shapes,
        in_specs=[SMEM_SPEC] * len(scalars)
        + [pl.BlockSpec(memory_space=pltpu.HBM)]
        + [VMEM_SPEC] * len(arrays),
        out_specs=jax.tree.map(lambda _: VMEM_SPEC, out_shapes),
        scratch_shapes=[
            *scratch,
            pltpu.VMEM(adjacency.shape, adjacency.dtype),
            pltpu.SemaphoreType.DMA((adjacency.shape[0] // CHUNK,)),
        ],
        compiler_params=pltpu.CompilerParams(vmem_limit_bytes=VMEM_LIMIT),
    )(
        *scalars,
        pltpu.with_memory_space_constraint(adjacency, pltpu.HBM),
        *(in_vmem(array) for array in arrays),
    )


def local(features, weight, grad_out, adjacency, tile_rows, tile_cols, tile_count):
    nodes, width = features.shape
    extent = adjacency.shape[1]
    rings, near, feats = (lax.axis_size(name) for name in ("ring", "near", "feat"))
    full = feats * width
    blocks = nodes // extent
    owners = near * feats
    swap = [(0, 1), (1, 0)]
    core, side, near_index = (
        lax.axis_index(name).astype(jnp.int32) for name in ("core", "side", "near")
    )
    table = jnp.concatenate([jnp.stack([core, side]), tile_count, tile_rows, tile_cols])
    bf16, f32 = jnp.bfloat16, jnp.float32

    def spread(value):
        copies = call(spread_kernel, (), (value,), pltpu.VMEM((rings, width, nodes), bf16))
        return lax.all_to_all(copies, "ring", 0, 0, tiled=False)

    own = features.T
    partner = lax.ppermute(own, "side", swap)
    same = spread(own)
    same, partner, table = lax.optimization_barrier((same, partner, table))
    far = spread(partner)

    half = jax.ShapeDtypeStruct((near, feats, width, extent), f32)
    keep, send = tile_call(
        forward_kernel,
        (table,),
        adjacency,
        (same, far),
        (half, half),
        [pltpu.VMEM((CORES * owners, width, extent), f32)],
    )
    received = lax.ppermute(send, "core", swap)
    flat = (owners, width, extent)
    terms = call(
        combine_kernel,
        (near_index.reshape(1),),
        (keep.reshape(flat), received.reshape(flat), weight),
        pltpu.VMEM((owners, width + PIECE, extent), bf16),
    )
    terms = lax.all_to_all(terms, ("near", "feat"), 0, 0, tiled=False)
    outgoing, activated = call(
        dense_kernel,
        (),
        (terms.reshape(near, feats, width + PIECE, extent), grad_out),
        (
            pltpu.VMEM((owners, width + PIECE, extent), bf16),
            jax.ShapeDtypeStruct((extent, full), bf16),
        ),
        [pltpu.VMEM((full, full), bf16)],
    )

    mine = lax.all_to_all(outgoing, ("near", "feat"), 0, 0, tiled=False)
    other = lax.ppermute(mine, "core", swap)
    pieces = tile_call(
        backward_kernel,
        (table,),
        adjacency,
        (mine, other),
        pltpu.VMEM((rings, SIDES * blocks * width + PIECE, extent), bf16),
        [
            pltpu.VMEM((near, CORES, feats, width, extent), bf16),
            pltpu.VMEM((rings * SIDES * blocks, width, extent), f32),
        ],
    )
    pieces = lax.all_to_all(pieces, "ring", 0, 0, tiled=False)
    block_sum = (blocks * width, extent)
    other_side, this_side, weight_piece = call(
        reduce_kernel,
        (),
        (pieces,),
        (
            pltpu.VMEM(block_sum, bf16),
            jax.ShapeDtypeStruct(block_sum, f32),
            pltpu.VMEM((SIDES * near, PIECE, extent), f32),
        ),
    )
    swapped = lax.ppermute(other_side, "side", swap)
    weight_terms = lax.all_to_all(weight_piece, ("side", "near"), 0, 0, tiled=False)
    scale = 1.0 / math.sqrt(nodes * rings * SIDES * near * CORES)
    feature_grad, weight_grad = call(
        lambda *refs: final_kernel(scale, *refs),
        (),
        (this_side, swapped, weight_terms),
        (
            jax.ShapeDtypeStruct((width, nodes), f32),
            jax.ShapeDtypeStruct((width, full), f32),
        ),
    )
    return (activated, weight_grad, feature_grad.T)


def solution(mesh):
    rows, cols, feats = (mesh.shape[name] for name in ("row", "col", "feat"))
    fine = jax.sharding.Mesh(
        mesh.devices.reshape(rows // SIDES, SIDES, cols // CORES, CORES, feats),
        ("ring", "side", "near", "core", "feat"),
    )
    pair = P(("ring", "side", "near", "core"))
    owner = P(("ring", "side", "near", "core", "feat"), None)
    by_column = P(("near", "core", "ring", "side"), "feat")
    return jax.shard_map(
        local,
        mesh=fine,
        in_specs=(by_column, P("feat", None), owner, pair, pair, pair, pair),
        out_specs=(owner, P("feat", None), by_column),
        check_vma=False,
    )
```

```python
import math

import jax
import jax.numpy as jnp
from jax import lax
from jax.experimental import pallas as pl
from jax.experimental.pallas import tpu as pltpu
from jax.sharding import PartitionSpec as P

CHUNK = 32
PIECE = 16
CORES = 2
SIDES = 2
HEAD = 3
VMEM_LIMIT = 24 * 1024 * 1024
NT = (((1,), (1,)), ((), ()))
NN = (((1,), (0,)), ((), ()))
TN = (((0,), (0,)), ((), ()))


def dot(a, b, dims):
    return lax.dot_general(a, b, dims, preferred_element_type=jnp.float32)


def stage_kernel(source_ref, out_ref, done):
    copy = pltpu.make_async_copy(source_ref, out_ref, done)
    copy.start()
    copy.wait()


def start_copies(adj_ref, tiles_ref, done):
    def load(chunk):
        part = pl.ds(chunk * CHUNK, CHUNK)
        return pltpu.make_async_copy(adj_ref.at[part], tiles_ref.at[part], done.at[chunk])

    for chunk in range(adj_ref.shape[0] // CHUNK):
        load(chunk).start()
    return lambda chunk: load(chunk).wait()


def accumulate_tiles(count, source, tiles_ref, wait, acc_ref, target_of, dims):
    chunks, extent = tiles_ref.shape[0] // CHUNK, tiles_ref.shape[1]
    acc_ref[...] = jnp.zeros_like(acc_ref)

    def product(slot):
        one, two = source(slot), source(slot + 1)
        zero = jnp.zeros_like(one)
        left = jnp.concatenate(
            [jnp.concatenate([one, zero], axis=1), jnp.concatenate([zero, two], axis=1)], axis=0
        )
        if dims is NN:
            right = tiles_ref[pl.ds(slot, 2)].reshape(2 * extent, extent)
        else:
            right = jnp.concatenate([tiles_ref[slot], tiles_ref[slot + 1]], axis=1)
        both = dot(left, right, dims)
        return both[: one.shape[0]], both[one.shape[0] :]

    @pl.loop(0, chunks)
    def _(chunk):
        wait(chunk)
        first = chunk * CHUNK

        @pl.when(first < count)
        def _():
            terms = [term for u in range(0, CHUNK, 2) for term in product(first + u)]
            for u, term in enumerate(terms):
                target = target_of(first + u)
                acc_ref[target] += jnp.where(first + u < count, term, 0.0)


def slots_of(table, slots):
    return lambda s: table[HEAD + s], lambda s: table[HEAD + slots + s]


def forward_kernel(
    table, adj_ref, same_ref, far_ref, keep_ref, send_ref, acc_ref, tiles_ref, done
):
    core, side, count = table[0], table[1], table[2]
    wait = start_copies(adj_ref, tiles_ref, done)
    slots, extent, _ = adj_ref.shape
    blocks = same_ref.shape[2] // extent
    row_of, col_of = slots_of(table, slots)

    def source(slot):
        col = col_of(slot)
        row_device = col // blocks
        nodes = pl.ds(pl.multiple_of((col % blocks) * extent, extent), extent)
        ring = row_device // SIDES
        return jnp.where(
            row_device % SIDES == side, same_ref[ring, :, nodes], far_ref[ring, :, nodes]
        )

    accumulate_tiles(count, source, tiles_ref, wait, acc_ref, row_of, NT)
    near, feats = keep_ref.shape[:2]
    for pair in range(near):
        keep_ref[pair] = acc_ref[pl.ds((pair * CORES + core) * feats, feats)]
        send_ref[pair] = acc_ref[pl.ds((pair * CORES + 1 - core) * feats, feats)]


def spread_kernel(value_ref, out_ref):
    for copy in range(out_ref.shape[0]):
        out_ref[copy] = value_ref[...]


def combine_kernel(near, keep_ref, received_ref, weight_ref, out_ref):
    owners, width, extent = keep_ref.shape
    halves = weight_ref.shape[1] // extent
    out_ref[:, :width] = (keep_ref[...] + received_ref[...]).astype(out_ref.dtype)
    top = pl.multiple_of((near[0] // halves) * PIECE, PIECE)
    left = pl.multiple_of((near[0] % halves) * extent, extent)
    piece = weight_ref[pl.ds(top, PIECE), pl.ds(left, extent)]
    for owner in range(owners):
        out_ref[owner, width:] = piece


def dense_kernel(terms_ref, grad_ref, out_ref, act_ref, weight_ref):
    near, feats, height, extent = terms_ref.shape
    width = height - PIECE
    full = feats * width
    halves = full // extent
    for pair in range(near):
        for feat in range(feats):
            top = feat * width + (pair // halves) * PIECE
            left = (pair % halves) * extent
            weight_ref[top : top + PIECE, left : left + extent] = terms_ref[pair, feat, width:]
    weight = weight_ref[...]
    summed = jnp.sum(terms_ref[:, :, :width].astype(jnp.float32), axis=0).reshape(full, extent)
    high = summed.astype(jnp.bfloat16)
    low = (summed - high.astype(jnp.float32)).astype(jnp.bfloat16)
    pre_act = dot(high, weight, TN) + dot(low, weight, TN)
    gate = jax.nn.sigmoid(pre_act)
    act_ref[...] = (pre_act * gate).astype(act_ref.dtype)
    derivative = gate * (1.0 + pre_act * (1.0 - gate))
    grad_pre = (grad_ref[...].astype(jnp.float32) * derivative).astype(jnp.bfloat16)
    projected = dot(weight, grad_pre, NT).astype(out_ref.dtype)
    weight_term = (dot(high, grad_pre, NN) + dot(low, grad_pre, NN)).astype(out_ref.dtype)
    for pair in range(near):
        for feat in range(feats):
            top = feat * width + (pair // halves) * PIECE
            left = (pair % halves) * extent
            out_ref[pair * feats + feat, :width] = projected[feat * width : (feat + 1) * width]
            out_ref[pair * feats + feat, width:] = weight_term[
                top : top + PIECE, left : left + extent
            ]


def backward_kernel(
    table, tiles_ref, mine_ref, other_ref, out_ref, proj_ref, acc_ref
):
    core, side, count = table[0], table[1], table[2]
    row_of, col_of = slots_of(table, tiles_ref.shape[0])
    rings = out_ref.shape[0]
    width = acc_ref.shape[1]
    blocks = acc_ref.shape[0] // (rings * SIDES)
    feats = proj_ref.shape[2]
    for pair in range(proj_ref.shape[0]):
        part = slice(pair * feats, (pair + 1) * feats)
        proj_ref[pair, core] = mine_ref[part, :width]
        proj_ref[pair, 1 - core] = other_ref[part, :width]

    def source(slot):
        row = row_of(slot)
        return proj_ref[row // (CORES * feats), (row // feats) % CORES, row % feats]

    accumulate_tiles(count, source, tiles_ref, lambda chunk: None, acc_ref, col_of, NN)
    weight_term = jnp.sum(mine_ref[:, width:].astype(jnp.float32), axis=0) + jnp.sum(
        other_ref[:, width:].astype(jnp.float32), axis=0
    )
    for ring in range(rings):
        for part, out_side in enumerate((1 - side, side)):
            start = (ring * SIDES + out_side) * blocks
            for block in range(blocks):
                top = (part * blocks + block) * width
                out_ref[ring, top : top + width] = acc_ref[start + block].astype(out_ref.dtype)
        for top in range(SIDES * blocks * width, out_ref.shape[1], PIECE):
            out_ref[ring, top : top + PIECE] = weight_term.astype(out_ref.dtype)


def reduce_kernel(pieces_ref, far_ref, same_ref, weight_ref):
    rows = far_ref.shape[0]
    far_ref[...] = jnp.sum(pieces_ref[:, :rows].astype(jnp.float32), axis=0).astype(far_ref.dtype)
    same_ref[...] = jnp.sum(pieces_ref[:, rows : 2 * rows].astype(jnp.float32), axis=0)
    weight_ref[...] = jnp.sum(
        pieces_ref[:, 2 * rows : 2 * rows + PIECE].astype(jnp.float32), axis=0
    )


def final_kernel(scale, same_ref, swapped_ref, terms_ref, grad_ref, weight_ref):
    width, nodes = grad_ref.shape
    extent = same_ref.shape[1]
    for block in range(nodes // extent):
        part = slice(block * width, (block + 1) * width)
        grad_ref[:, block * extent : (block + 1) * extent] = same_ref[part] + swapped_ref[
            part
        ].astype(jnp.float32)
    halves = weight_ref.shape[1] // extent
    near = terms_ref.shape[0] // SIDES
    for pair in range(near):
        top, left = (pair // halves) * PIECE, (pair % halves) * extent
        weight_ref[top : top + PIECE, left : left + extent] = (
            terms_ref[pair] + terms_ref[near + pair]
        ) * scale


SMEM_SPEC = pl.BlockSpec(memory_space=pltpu.SMEM)
VMEM_SPEC = pl.BlockSpec(memory_space=pltpu.VMEM)


def in_vmem(array):
    return pltpu.with_memory_space_constraint(array, pltpu.VMEM)


def call(kernel, scalars, arrays, out_shapes, scratch=()):
    return pl.pallas_call(
        kernel,
        out_shape=out_shapes,
        in_specs=[SMEM_SPEC] * len(scalars) + [VMEM_SPEC] * len(arrays),
        out_specs=jax.tree.map(lambda _: VMEM_SPEC, out_shapes),
        scratch_shapes=scratch,
        compiler_params=pltpu.CompilerParams(vmem_limit_bytes=VMEM_LIMIT),
    )(*scalars, *(in_vmem(array) for array in arrays))


def stage(array):
    return pl.pallas_call(
        stage_kernel,
        out_shape=pltpu.VMEM(array.shape, array.dtype),
        in_specs=[pl.BlockSpec(memory_space=pltpu.HBM)],
        out_specs=VMEM_SPEC,
        scratch_shapes=[pltpu.SemaphoreType.DMA],
        compiler_params=pltpu.CompilerParams(vmem_limit_bytes=VMEM_LIMIT),
    )(pltpu.with_memory_space_constraint(array, pltpu.HBM))


def tile_call(kernel, scalars, adjacency, arrays, out_shapes, scratch):
    return pl.pallas_call(
        kernel,
        out_shape=out_shapes,
        in_specs=[SMEM_SPEC] * len(scalars)
        + [pl.BlockSpec(memory_space=pltpu.HBM)]
        + [VMEM_SPEC] * len(arrays),
        out_specs=jax.tree.map(lambda _: VMEM_SPEC, out_shapes),
        scratch_shapes=[
            *scratch,
            pltpu.VMEM(adjacency.shape, adjacency.dtype),
            pltpu.SemaphoreType.DMA((adjacency.shape[0] // CHUNK,)),
        ],
        compiler_params=pltpu.CompilerParams(vmem_limit_bytes=VMEM_LIMIT),
    )(
        *scalars,
        pltpu.with_memory_space_constraint(adjacency, pltpu.HBM),
        *(in_vmem(array) for array in arrays),
    )


def local(features, weight, grad_out, adjacency, tile_rows, tile_cols, tile_count):
    nodes, width = features.shape
    extent = adjacency.shape[1]
    rings, near, feats = (lax.axis_size(name) for name in ("ring", "near", "feat"))
    full = feats * width
    blocks = nodes // extent
    owners = near * feats
    swap = [(0, 1), (1, 0)]
    core, side, near_index = (
        lax.axis_index(name).astype(jnp.int32) for name in ("core", "side", "near")
    )
    table = jnp.concatenate([jnp.stack([core, side]), tile_count, tile_rows, tile_cols])
    bf16, f32 = jnp.bfloat16, jnp.float32

    def spread(value):
        copies = call(spread_kernel, (), (value,), pltpu.VMEM((rings, width, nodes), bf16))
        return lax.all_to_all(copies, "ring", 0, 0, tiled=False)

    own = features.T
    partner = lax.ppermute(own, "side", swap)
    same = spread(own)
    same, partner, table = lax.optimization_barrier((same, partner, table))
    far = spread(partner)

    half = jax.ShapeDtypeStruct((near, feats, width, extent), f32)
    keep, send = tile_call(
        forward_kernel,
        (table,),
        adjacency,
        (same, far),
        (half, half),
        [pltpu.VMEM((CORES * owners, width, extent), f32)],
    )
    received = lax.ppermute(send, "core", swap)
    flat = (owners, width, extent)
    terms = call(
        combine_kernel,
        (near_index.reshape(1),),
        (keep.reshape(flat), received.reshape(flat), weight),
        pltpu.VMEM((owners, width + PIECE, extent), bf16),
    )
    terms = lax.all_to_all(terms, ("near", "feat"), 0, 0, tiled=False)
    outgoing, activated = call(
        dense_kernel,
        (),
        (terms.reshape(near, feats, width + PIECE, extent), grad_out),
        (
            pltpu.VMEM((owners, width + PIECE, extent), bf16),
            jax.ShapeDtypeStruct((extent, full), bf16),
        ),
        [pltpu.VMEM((full, full), bf16)],
    )

    mine = lax.all_to_all(outgoing, ("near", "feat"), 0, 0, tiled=False)
    mine, adjacency = lax.optimization_barrier((mine, adjacency))
    other = lax.ppermute(mine, "core", swap)
    pieces = call(
        backward_kernel,
        (table,),
        (stage(adjacency), mine, other),
        pltpu.VMEM((rings, SIDES * blocks * width + 2 * PIECE, extent), bf16),
        [
            pltpu.VMEM((near, CORES, feats, width, extent), bf16),
            pltpu.VMEM((rings * SIDES * blocks, width, extent), f32),
        ],
    )
    pieces = lax.all_to_all(pieces, "ring", 0, 0, tiled=False)
    block_sum = (blocks * width, extent)
    other_side, this_side, weight_piece = call(
        reduce_kernel,
        (),
        (pieces,),
        (
            pltpu.VMEM(block_sum, bf16),
            jax.ShapeDtypeStruct(block_sum, f32),
            pltpu.VMEM((PIECE, extent), f32),
        ),
    )
    weight_piece = call(
        spread_kernel, (), (weight_piece,), pltpu.VMEM((SIDES * near, PIECE, extent), f32)
    )
    swapped = lax.ppermute(other_side, "side", swap)
    weight_terms = lax.all_to_all(weight_piece, ("side", "near"), 0, 0, tiled=False)
    scale = 1.0 / math.sqrt(nodes * rings * SIDES * near * CORES)
    feature_grad, weight_grad = call(
        lambda *refs: final_kernel(scale, *refs),
        (),
        (this_side, swapped, weight_terms),
        (
            jax.ShapeDtypeStruct((width, nodes), f32),
            jax.ShapeDtypeStruct((width, full), f32),
        ),
    )
    return (activated, weight_grad, feature_grad.T)


def solution(mesh):
    rows, cols, feats = (mesh.shape[name] for name in ("row", "col", "feat"))
    fine = jax.sharding.Mesh(
        mesh.devices.reshape(rows // SIDES, SIDES, cols // CORES, CORES, feats),
        ("ring", "side", "near", "core", "feat"),
    )
    pair = P(("ring", "side", "near", "core"))
    owner = P(("ring", "side", "near", "core", "feat"), None)
    by_column = P(("near", "core", "ring", "side"), "feat")
    return jax.shard_map(
        local,
        mesh=fine,
        in_specs=(by_column, P("feat", None), owner, pair, pair, pair, pair),
        out_specs=(owner, P("feat", None), by_column),
        check_vma=False,
    )
```

```python
import math

import jax
import jax.numpy as jnp
from jax import lax
from jax.experimental import pallas as pl
from jax.experimental.pallas import tpu as pltpu
from jax.sharding import PartitionSpec as P

CHUNK = 32
PIECE = 16
CORES = 2
SIDES = 2
HEAD = 3
VMEM_LIMIT = 24 * 1024 * 1024
NT = (((1,), (1,)), ((), ()))
NN = (((1,), (0,)), ((), ()))
TN = (((0,), (0,)), ((), ()))


def dot(a, b, dims):
    return lax.dot_general(a, b, dims, preferred_element_type=jnp.float32)


def accumulate_tiles(count, source, adj_ref, tiles_ref, done, acc_ref, target_of, dims):
    chunks, extent = adj_ref.shape[0] // CHUNK, adj_ref.shape[1]

    def load(chunk):
        part = pl.ds(chunk * CHUNK, CHUNK)
        return pltpu.make_async_copy(adj_ref.at[part], tiles_ref.at[part], done.at[chunk])

    for chunk in range(chunks):
        load(chunk).start()
    acc_ref[...] = jnp.zeros_like(acc_ref)

    def product(slot):
        one, two = source(slot), source(slot + 1)
        zero = jnp.zeros_like(one)
        left = jnp.concatenate(
            [jnp.concatenate([one, zero], axis=1), jnp.concatenate([zero, two], axis=1)], axis=0
        )
        if dims is NN:
            right = tiles_ref[pl.ds(slot, 2)].reshape(2 * extent, extent)
        else:
            right = jnp.concatenate([tiles_ref[slot], tiles_ref[slot + 1]], axis=1)
        both = dot(left, right, dims)
        return both[: one.shape[0]], both[one.shape[0] :]

    @pl.loop(0, chunks)
    def _(chunk):
        load(chunk).wait()
        first = chunk * CHUNK

        @pl.when(first < count)
        def _():
            terms = [term for u in range(0, CHUNK, 2) for term in product(first + u)]
            for u, term in enumerate(terms):
                target = target_of(first + u)
                acc_ref[target] += jnp.where(first + u < count, term, 0.0)


def slots_of(table, slots):
    return lambda s: table[HEAD + s], lambda s: table[HEAD + slots + s]


def forward_kernel(table, adj_ref, feat_ref, keep_ref, send_ref, acc_ref, *tiles):
    core, count = table[0], table[2]
    slots, extent, _ = adj_ref.shape
    blocks = feat_ref.shape[2] // extent
    row_of, col_of = slots_of(table, slots)

    def source(slot):
        col = col_of(slot)
        nodes = pl.ds(pl.multiple_of((col % blocks) * extent, extent), extent)
        return feat_ref[col // blocks, :, nodes]

    accumulate_tiles(count, source, adj_ref, *tiles, acc_ref, row_of, NT)
    near, feats = keep_ref.shape[:2]
    for pair in range(near):
        keep_ref[pair] = acc_ref[pl.ds((pair * CORES + core) * feats, feats)]
        send_ref[pair] = acc_ref[pl.ds((pair * CORES + 1 - core) * feats, feats)]


def spread_kernel(value_ref, out_ref):
    for copy in range(out_ref.shape[0]):
        out_ref[copy] = value_ref[...]


def combine_kernel(near, keep_ref, received_ref, weight_ref, out_ref):
    owners, width, extent = keep_ref.shape
    halves = weight_ref.shape[1] // extent
    out_ref[:, :width] = (keep_ref[...] + received_ref[...]).astype(out_ref.dtype)
    top = pl.multiple_of((near[0] // halves) * PIECE, PIECE)
    left = pl.multiple_of((near[0] % halves) * extent, extent)
    piece = weight_ref[pl.ds(top, PIECE), pl.ds(left, extent)]
    for owner in range(owners):
        out_ref[owner, width:] = piece


def dense_kernel(terms_ref, grad_ref, out_ref, act_ref, weight_ref):
    near, feats, height, extent = terms_ref.shape
    width = height - PIECE
    full = feats * width
    halves = full // extent
    for pair in range(near):
        for feat in range(feats):
            top = feat * width + (pair // halves) * PIECE
            left = (pair % halves) * extent
            weight_ref[top : top + PIECE, left : left + extent] = terms_ref[pair, feat, width:]
    weight = weight_ref[...]
    summed = jnp.sum(terms_ref[:, :, :width].astype(jnp.float32), axis=0).reshape(full, extent)
    high = summed.astype(jnp.bfloat16)
    low = (summed - high.astype(jnp.float32)).astype(jnp.bfloat16)
    pre_act = dot(high, weight, TN) + dot(low, weight, TN)
    gate = jax.nn.sigmoid(pre_act)
    act_ref[...] = (pre_act * gate).astype(act_ref.dtype)
    derivative = gate * (1.0 + pre_act * (1.0 - gate))
    grad_pre = (grad_ref[...].astype(jnp.float32) * derivative).astype(jnp.bfloat16)
    projected = dot(weight, grad_pre, NT).astype(out_ref.dtype)
    weight_term = (dot(high, grad_pre, NN) + dot(low, grad_pre, NN)).astype(out_ref.dtype)
    for pair in range(near):
        for feat in range(feats):
            top = feat * width + (pair // halves) * PIECE
            left = (pair % halves) * extent
            out_ref[pair * feats + feat, :width] = projected[feat * width : (feat + 1) * width]
            out_ref[pair * feats + feat, width:] = weight_term[
                top : top + PIECE, left : left + extent
            ]


def backward_kernel(
    table, adj_ref, mine_ref, other_ref, out_ref, proj_ref, acc_ref, *tiles
):
    core, side, count = table[0], table[1], table[2]
    row_of, col_of = slots_of(table, adj_ref.shape[0])
    rings = out_ref.shape[0]
    width = acc_ref.shape[1]
    blocks = acc_ref.shape[0] // (rings * SIDES)
    feats = proj_ref.shape[2]
    for pair in range(proj_ref.shape[0]):
        part = slice(pair * feats, (pair + 1) * feats)
        proj_ref[pair, core] = mine_ref[part, :width]
        proj_ref[pair, 1 - core] = other_ref[part, :width]

    def source(slot):
        row = row_of(slot)
        return proj_ref[row // (CORES * feats), (row // feats) % CORES, row % feats]

    accumulate_tiles(count, source, adj_ref, *tiles, acc_ref, col_of, NN)
    weight_term = jnp.sum(mine_ref[:, width:].astype(jnp.float32), axis=0) + jnp.sum(
        other_ref[:, width:].astype(jnp.float32), axis=0
    )
    for ring in range(rings):
        for part, out_side in enumerate((1 - side, side)):
            start = (ring * SIDES + out_side) * blocks
            for block in range(blocks):
                top = (part * blocks + block) * width
                out_ref[ring, top : top + width] = acc_ref[start + block].astype(out_ref.dtype)
        out_ref[ring, SIDES * blocks * width :] = weight_term.astype(out_ref.dtype)


def reduce_kernel(pieces_ref, far_ref, same_ref, weight_ref):
    rows = far_ref.shape[0]
    far_ref[...] = jnp.sum(pieces_ref[:, :rows].astype(jnp.float32), axis=0).astype(far_ref.dtype)
    same_ref[...] = jnp.sum(pieces_ref[:, rows : 2 * rows].astype(jnp.float32), axis=0)
    weight_term = jnp.sum(pieces_ref[:, 2 * rows :].astype(jnp.float32), axis=0)
    for copy in range(weight_ref.shape[0]):
        weight_ref[copy] = weight_term


def final_kernel(scale, same_ref, swapped_ref, terms_ref, grad_ref, weight_ref):
    width, nodes = grad_ref.shape
    extent = same_ref.shape[1]
    for block in range(nodes // extent):
        part = slice(block * width, (block + 1) * width)
        grad_ref[:, block * extent : (block + 1) * extent] = same_ref[part] + swapped_ref[
            part
        ].astype(jnp.float32)
    halves = weight_ref.shape[1] // extent
    near = terms_ref.shape[0] // SIDES
    for pair in range(near):
        top, left = (pair // halves) * PIECE, (pair % halves) * extent
        weight_ref[top : top + PIECE, left : left + extent] = (
            terms_ref[pair] + terms_ref[near + pair]
        ) * scale


SMEM_SPEC = pl.BlockSpec(memory_space=pltpu.SMEM)
VMEM_SPEC = pl.BlockSpec(memory_space=pltpu.VMEM)


def in_vmem(array):
    return pltpu.with_memory_space_constraint(array, pltpu.VMEM)


def call(kernel, scalars, arrays, out_shapes, scratch=()):
    return pl.pallas_call(
        kernel,
        out_shape=out_shapes,
        in_specs=[SMEM_SPEC] * len(scalars) + [VMEM_SPEC] * len(arrays),
        out_specs=jax.tree.map(lambda _: VMEM_SPEC, out_shapes),
        scratch_shapes=scratch,
        compiler_params=pltpu.CompilerParams(vmem_limit_bytes=VMEM_LIMIT),
    )(*scalars, *(in_vmem(array) for array in arrays))


def tile_call(kernel, scalars, adjacency, arrays, out_shapes, scratch):
    return pl.pallas_call(
        kernel,
        out_shape=out_shapes,
        in_specs=[SMEM_SPEC] * len(scalars)
        + [pl.BlockSpec(memory_space=pltpu.HBM)]
        + [VMEM_SPEC] * len(arrays),
        out_specs=jax.tree.map(lambda _: VMEM_SPEC, out_shapes),
        scratch_shapes=[
            *scratch,
            pltpu.VMEM(adjacency.shape, adjacency.dtype),
            pltpu.SemaphoreType.DMA((adjacency.shape[0] // CHUNK,)),
        ],
        compiler_params=pltpu.CompilerParams(vmem_limit_bytes=VMEM_LIMIT),
    )(
        *scalars,
        pltpu.with_memory_space_constraint(adjacency, pltpu.HBM),
        *(in_vmem(array) for array in arrays),
    )


def local(features, weight, grad_out, adjacency, tile_rows, tile_cols, tile_count):
    nodes, width = features.shape
    extent = adjacency.shape[1]
    rings, near, feats = (lax.axis_size(name) for name in ("ring", "near", "feat"))
    full = feats * width
    blocks = nodes // extent
    owners = near * feats
    swap = [(0, 1), (1, 0)]
    core, side, near_index = (
        lax.axis_index(name).astype(jnp.int32) for name in ("core", "side", "near")
    )
    table = jnp.concatenate([jnp.stack([core, side]), tile_count, tile_rows, tile_cols])
    bf16, f32 = jnp.bfloat16, jnp.float32

    own = call(
        spread_kernel, (), (features.T,), pltpu.VMEM((rings * SIDES, width, nodes), bf16)
    )
    own, table = lax.optimization_barrier((own, table))
    gathered = lax.all_to_all(own, ("ring", "side"), 0, 0, tiled=False)

    half = jax.ShapeDtypeStruct((near, feats, width, extent), f32)
    keep, send = tile_call(
        forward_kernel,
        (table,),
        adjacency,
        (gathered,),
        (half, half),
        [pltpu.VMEM((CORES * owners, width, extent), f32)],
    )
    received = lax.ppermute(send, "core", swap)
    flat = (owners, width, extent)
    terms = call(
        combine_kernel,
        (near_index.reshape(1),),
        (keep.reshape(flat), received.reshape(flat), weight),
        pltpu.VMEM((owners, width + PIECE, extent), bf16),
    )
    terms = lax.all_to_all(terms, ("near", "feat"), 0, 0, tiled=False)
    outgoing, activated = call(
        dense_kernel,
        (),
        (terms.reshape(near, feats, width + PIECE, extent), grad_out),
        (
            pltpu.VMEM((owners, width + PIECE, extent), bf16),
            jax.ShapeDtypeStruct((extent, full), bf16),
        ),
        [pltpu.VMEM((full, full), bf16)],
    )

    mine = lax.all_to_all(outgoing, ("near", "feat"), 0, 0, tiled=False)
    other = lax.ppermute(mine, "core", swap)
    pieces = tile_call(
        backward_kernel,
        (table,),
        adjacency,
        (mine, other),
        pltpu.VMEM((rings, SIDES * blocks * width + PIECE, extent), bf16),
        [
            pltpu.VMEM((near, CORES, feats, width, extent), bf16),
            pltpu.VMEM((rings * SIDES * blocks, width, extent), f32),
        ],
    )
    pieces = lax.all_to_all(pieces, "ring", 0, 0, tiled=False)
    block_sum = (blocks * width, extent)
    other_side, this_side, weight_piece = call(
        reduce_kernel,
        (),
        (pieces,),
        (
            jax.ShapeDtypeStruct(block_sum, f32),
            jax.ShapeDtypeStruct(block_sum, f32),
            pltpu.VMEM((SIDES * near, PIECE, extent), f32),
        ),
    )
    swapped = lax.ppermute(other_side, "side", swap)
    weight_terms = lax.all_to_all(weight_piece, ("side", "near"), 0, 0, tiled=False)
    scale = 1.0 / math.sqrt(nodes * rings * SIDES * near * CORES)
    feature_grad, weight_grad = call(
        lambda *refs: final_kernel(scale, *refs),
        (),
        (this_side, swapped, weight_terms),
        (
            jax.ShapeDtypeStruct((width, nodes), f32),
            jax.ShapeDtypeStruct((width, full), f32),
        ),
    )
    return (activated, weight_grad, feature_grad.T)


def solution(mesh):
    rows, cols, feats = (mesh.shape[name] for name in ("row", "col", "feat"))
    fine = jax.sharding.Mesh(
        mesh.devices.reshape(rows // SIDES, SIDES, cols // CORES, CORES, feats),
        ("ring", "side", "near", "core", "feat"),
    )
    pair = P(("ring", "side", "near", "core"))
    owner = P(("ring", "side", "near", "core", "feat"), None)
    by_column = P(("near", "core", "ring", "side"), "feat")
    return jax.shard_map(
        local,
        mesh=fine,
        in_specs=(by_column, P("feat", None), owner, pair, pair, pair, pair),
        out_specs=(owner, P("feat", None), by_column),
        check_vma=False,
    )
```

```python
import math

import jax
import jax.numpy as jnp
from jax import lax
from jax.experimental import pallas as pl
from jax.experimental.pallas import tpu as pltpu
from jax.sharding import PartitionSpec as P

CHUNK = 32
PIECE = 16
CORES = 2
SIDES = 2
HEAD = 3
VMEM_LIMIT = 24 * 1024 * 1024
NT = (((1,), (1,)), ((), ()))
NN = (((1,), (0,)), ((), ()))
TN = (((0,), (0,)), ((), ()))


def dot(a, b, dims):
    return lax.dot_general(a, b, dims, preferred_element_type=jnp.float32)


def accumulate_tiles(count, gather, source, adj_ref, tiles_ref, done, acc_ref, target_of, dims):
    chunks, extent = adj_ref.shape[0] // CHUNK, adj_ref.shape[1]

    def load(chunk):
        part = pl.ds(chunk * CHUNK, CHUNK)
        return pltpu.make_async_copy(adj_ref.at[part], tiles_ref.at[part], done.at[chunk])

    for chunk in range(chunks):
        load(chunk).start()
    gather()
    acc_ref[...] = jnp.zeros_like(acc_ref)

    def product(slot):
        one, two = source(slot), source(slot + 1)
        zero = jnp.zeros_like(one)
        left = jnp.concatenate(
            [jnp.concatenate([one, zero], axis=1), jnp.concatenate([zero, two], axis=1)], axis=0
        )
        if dims is NN:
            right = tiles_ref[pl.ds(slot, 2)].reshape(2 * extent, extent)
        else:
            right = jnp.concatenate([tiles_ref[slot], tiles_ref[slot + 1]], axis=1)
        both = dot(left, right, dims)
        return both[: one.shape[0]], both[one.shape[0] :]

    @pl.loop(0, chunks)
    def _(chunk):
        load(chunk).wait()
        first = chunk * CHUNK

        @pl.when(first < count)
        def _():
            terms = [term for u in range(0, CHUNK, 2) for term in product(first + u)]
            for u, term in enumerate(terms):
                target = target_of(first + u)
                acc_ref[target] += jnp.where(first + u < count, term, 0.0)


def slots_of(table, slots):
    return lambda s: table[HEAD + s], lambda s: table[HEAD + slots + s]


def forward_kernel(
    table, adj_ref, same_ref, far_ref, keep_ref, send_ref, feat_ref, acc_ref, *tiles
):
    core, side, count = table[0], table[1], table[2]
    slots, extent, _ = adj_ref.shape
    blocks = same_ref.shape[2] // extent
    row_of, col_of = slots_of(table, slots)

    def source(slot):
        col = col_of(slot)
        nodes = pl.ds(pl.multiple_of((col % blocks) * extent, extent), extent)
        return feat_ref[col // blocks, :, nodes]

    def gather():
        for ring in range(same_ref.shape[0]):
            feat_ref[ring * SIDES + side] = same_ref[ring]
            feat_ref[ring * SIDES + 1 - side] = far_ref[ring]

    accumulate_tiles(count, gather, source, adj_ref, *tiles, acc_ref, row_of, NT)
    near, feats = keep_ref.shape[:2]
    for pair in range(near):
        keep_ref[pair] = acc_ref[pl.ds((pair * CORES + core) * feats, feats)]
        send_ref[pair] = acc_ref[pl.ds((pair * CORES + 1 - core) * feats, feats)]


def spread_kernel(value_ref, out_ref):
    for copy in range(out_ref.shape[0]):
        out_ref[copy] = value_ref[...]


def combine_kernel(near, keep_ref, received_ref, weight_ref, out_ref):
    owners, width, extent = keep_ref.shape
    halves = weight_ref.shape[1] // extent
    out_ref[:, :width] = (keep_ref[...] + received_ref[...]).astype(out_ref.dtype)
    top = pl.multiple_of((near[0] // halves) * PIECE, PIECE)
    left = pl.multiple_of((near[0] % halves) * extent, extent)
    piece = weight_ref[pl.ds(top, PIECE), pl.ds(left, extent)]
    for owner in range(owners):
        out_ref[owner, width:] = piece


def dense_kernel(terms_ref, grad_ref, out_ref, act_ref, weight_ref):
    near, feats, height, extent = terms_ref.shape
    width = height - PIECE
    full = feats * width
    halves = full // extent
    for pair in range(near):
        for feat in range(feats):
            top = feat * width + (pair // halves) * PIECE
            left = (pair % halves) * extent
            weight_ref[top : top + PIECE, left : left + extent] = terms_ref[pair, feat, width:]
    weight = weight_ref[...]
    summed = jnp.sum(terms_ref[:, :, :width].astype(jnp.float32), axis=0).reshape(full, extent)
    high = summed.astype(jnp.bfloat16)
    low = (summed - high.astype(jnp.float32)).astype(jnp.bfloat16)
    pre_act = dot(high, weight, TN) + dot(low, weight, TN)
    gate = jax.nn.sigmoid(pre_act)
    act_ref[...] = (pre_act * gate).astype(act_ref.dtype)
    derivative = gate * (1.0 + pre_act * (1.0 - gate))
    grad_pre = (grad_ref[...].astype(jnp.float32) * derivative).astype(jnp.bfloat16)
    projected = dot(weight, grad_pre, NT).astype(out_ref.dtype)
    weight_term = (dot(high, grad_pre, NN) + dot(low, grad_pre, NN)).astype(out_ref.dtype)
    for pair in range(near):
        for feat in range(feats):
            top = feat * width + (pair // halves) * PIECE
            left = (pair % halves) * extent
            out_ref[pair * feats + feat, :width] = projected[feat * width : (feat + 1) * width]
            out_ref[pair * feats + feat, width:] = weight_term[
                top : top + PIECE, left : left + extent
            ]


def backward_kernel(
    table, adj_ref, mine_ref, other_ref, out_ref, proj_ref, acc_ref, *tiles
):
    core, side, count = table[0], table[1], table[2]
    row_of, col_of = slots_of(table, adj_ref.shape[0])
    rings = out_ref.shape[0]
    width = acc_ref.shape[1]
    blocks = acc_ref.shape[0] // (rings * SIDES)
    feats = proj_ref.shape[2]

    def gather():
        for pair in range(proj_ref.shape[0]):
            part = slice(pair * feats, (pair + 1) * feats)
            proj_ref[pair, core] = mine_ref[part, :width]
            proj_ref[pair, 1 - core] = other_ref[part, :width]

    def source(slot):
        row = row_of(slot)
        return proj_ref[row // (CORES * feats), (row // feats) % CORES, row % feats]

    accumulate_tiles(count, gather, source, adj_ref, *tiles, acc_ref, col_of, NN)
    weight_term = jnp.sum(mine_ref[:, width:].astype(jnp.float32), axis=0) + jnp.sum(
        other_ref[:, width:].astype(jnp.float32), axis=0
    )
    for ring in range(rings):
        for part, out_side in enumerate((1 - side, side)):
            start = (ring * SIDES + out_side) * blocks
            for block in range(blocks):
                top = (part * blocks + block) * width
                out_ref[ring, top : top + width] = acc_ref[start + block].astype(out_ref.dtype)
        out_ref[ring, SIDES * blocks * width :] = weight_term.astype(out_ref.dtype)


def reduce_kernel(pieces_ref, far_ref, same_ref, weight_ref):
    rows = far_ref.shape[0]
    far_ref[...] = jnp.sum(pieces_ref[:, :rows].astype(jnp.float32), axis=0)
    same_ref[...] = jnp.sum(pieces_ref[:, rows : 2 * rows].astype(jnp.float32), axis=0)
    weight_term = jnp.sum(pieces_ref[:, 2 * rows :].astype(jnp.float32), axis=0)
    for copy in range(weight_ref.shape[0]):
        weight_ref[copy] = weight_term


def final_kernel(scale, same_ref, swapped_ref, terms_ref, grad_ref, weight_ref):
    width, nodes = grad_ref.shape
    extent = same_ref.shape[1]
    for block in range(nodes // extent):
        part = slice(block * width, (block + 1) * width)
        grad_ref[:, block * extent : (block + 1) * extent] = same_ref[part] + swapped_ref[part]
    halves = weight_ref.shape[1] // extent
    near = terms_ref.shape[0] // SIDES
    for pair in range(near):
        top, left = (pair // halves) * PIECE, (pair % halves) * extent
        weight_ref[top : top + PIECE, left : left + extent] = (
            terms_ref[pair] + terms_ref[near + pair]
        ) * scale


SMEM_SPEC = pl.BlockSpec(memory_space=pltpu.SMEM)
VMEM_SPEC = pl.BlockSpec(memory_space=pltpu.VMEM)


def in_vmem(array):
    return pltpu.with_memory_space_constraint(array, pltpu.VMEM)


def call(kernel, scalars, arrays, out_shapes, scratch=()):
    return pl.pallas_call(
        kernel,
        out_shape=out_shapes,
        in_specs=[SMEM_SPEC] * len(scalars) + [VMEM_SPEC] * len(arrays),
        out_specs=jax.tree.map(lambda _: VMEM_SPEC, out_shapes),
        scratch_shapes=scratch,
        compiler_params=pltpu.CompilerParams(vmem_limit_bytes=VMEM_LIMIT),
    )(*scalars, *(in_vmem(array) for array in arrays))


def tile_call(kernel, scalars, adjacency, arrays, out_shapes, scratch):
    return pl.pallas_call(
        kernel,
        out_shape=out_shapes,
        in_specs=[SMEM_SPEC] * len(scalars)
        + [pl.BlockSpec(memory_space=pltpu.HBM)]
        + [VMEM_SPEC] * len(arrays),
        out_specs=jax.tree.map(lambda _: VMEM_SPEC, out_shapes),
        scratch_shapes=[
            *scratch,
            pltpu.VMEM(adjacency.shape, adjacency.dtype),
            pltpu.SemaphoreType.DMA((adjacency.shape[0] // CHUNK,)),
        ],
        compiler_params=pltpu.CompilerParams(vmem_limit_bytes=VMEM_LIMIT),
    )(
        *scalars,
        pltpu.with_memory_space_constraint(adjacency, pltpu.HBM),
        *(in_vmem(array) for array in arrays),
    )


def local(features, weight, grad_out, adjacency, tile_rows, tile_cols, tile_count):
    nodes, width = features.shape
    extent = adjacency.shape[1]
    rings, near, feats = (lax.axis_size(name) for name in ("ring", "near", "feat"))
    full = feats * width
    blocks = nodes // extent
    owners = near * feats
    swap = [(0, 1), (1, 0)]
    core, side, near_index = (
        lax.axis_index(name).astype(jnp.int32) for name in ("core", "side", "near")
    )
    table = jnp.concatenate([jnp.stack([core, side]), tile_count, tile_rows, tile_cols])
    bf16, f32 = jnp.bfloat16, jnp.float32

    def spread(value):
        copies = call(spread_kernel, (), (value,), pltpu.VMEM((rings, width, nodes), bf16))
        return lax.all_to_all(copies, "ring", 0, 0, tiled=False)

    own = features.T
    partner = lax.ppermute(own, "side", swap)
    same = spread(own)
    same, partner, table = lax.optimization_barrier((same, partner, table))
    far = spread(partner)

    half = jax.ShapeDtypeStruct((near, feats, width, extent), f32)
    keep, send = tile_call(
        forward_kernel,
        (table,),
        adjacency,
        (same, far),
        (half, half),
        [
            pltpu.VMEM((rings * SIDES, width, nodes), bf16),
            pltpu.VMEM((CORES * owners, width, extent), f32),
        ],
    )
    received = lax.ppermute(send, "core", swap)
    flat = (owners, width, extent)
    terms = call(
        combine_kernel,
        (near_index.reshape(1),),
        (keep.reshape(flat), received.reshape(flat), weight),
        pltpu.VMEM((owners, width + PIECE, extent), bf16),
    )
    terms = lax.all_to_all(terms, ("near", "feat"), 0, 0, tiled=False)
    outgoing, activated = call(
        dense_kernel,
        (),
        (terms.reshape(near, feats, width + PIECE, extent), grad_out),
        (
            pltpu.VMEM((owners, width + PIECE, extent), bf16),
            jax.ShapeDtypeStruct((extent, full), bf16),
        ),
        [pltpu.VMEM((full, full), bf16)],
    )

    mine = lax.all_to_all(outgoing, ("near", "feat"), 0, 0, tiled=False)
    other = lax.ppermute(mine, "core", swap)
    pieces = tile_call(
        backward_kernel,
        (table,),
        adjacency,
        (mine, other),
        pltpu.VMEM((rings, SIDES * blocks * width + PIECE, extent), bf16),
        [
            pltpu.VMEM((near, CORES, feats, width, extent), bf16),
            pltpu.VMEM((rings * SIDES * blocks, width, extent), f32),
        ],
    )
    pieces = lax.all_to_all(pieces, "ring", 0, 0, tiled=False)
    block_sum = (blocks * width, extent)
    other_side, this_side, weight_piece = call(
        reduce_kernel,
        (),
        (pieces,),
        (
            jax.ShapeDtypeStruct(block_sum, f32),
            jax.ShapeDtypeStruct(block_sum, f32),
            pltpu.VMEM((SIDES * near, PIECE, extent), f32),
        ),
    )
    swapped = lax.ppermute(other_side, "side", swap)
    weight_terms = lax.all_to_all(weight_piece, ("side", "near"), 0, 0, tiled=False)
    scale = 1.0 / math.sqrt(nodes * rings * SIDES * near * CORES)
    feature_grad, weight_grad = call(
        lambda *refs: final_kernel(scale, *refs),
        (),
        (this_side, swapped, weight_terms),
        (
            jax.ShapeDtypeStruct((width, nodes), f32),
            jax.ShapeDtypeStruct((width, full), f32),
        ),
    )
    return (activated, weight_grad, feature_grad.T)


def solution(mesh):
    rows, cols, feats = (mesh.shape[name] for name in ("row", "col", "feat"))
    fine = jax.sharding.Mesh(
        mesh.devices.reshape(rows // SIDES, SIDES, cols // CORES, CORES, feats),
        ("ring", "side", "near", "core", "feat"),
    )
    pair = P(("ring", "side", "near", "core"))
    owner = P(("ring", "side", "near", "core", "feat"), None)
    by_column = P(("near", "core", "ring", "side"), "feat")
    return jax.shard_map(
        local,
        mesh=fine,
        in_specs=(by_column, P("feat", None), owner, pair, pair, pair, pair),
        out_specs=(owner, P("feat", None), by_column),
        check_vma=False,
    )
```

```python
import math

import jax
import jax.numpy as jnp
from jax import lax
from jax.experimental import pallas as pl
from jax.experimental.pallas import tpu as pltpu
from jax.sharding import PartitionSpec as P

CHUNK = 32
PIECE = 16
CORES = 2
SIDES = 2
HEAD = 3
VMEM_LIMIT = 24 * 1024 * 1024
NT = (((1,), (1,)), ((), ()))
NN = (((1,), (0,)), ((), ()))
TN = (((0,), (0,)), ((), ()))


def dot(a, b, dims):
    return lax.dot_general(a, b, dims, preferred_element_type=jnp.float32)


def accumulate_tiles(count, gather, source, adj_ref, tiles_ref, done, acc_ref, target_of, dims):
    chunks, extent = adj_ref.shape[0] // CHUNK, adj_ref.shape[1]

    def load(chunk):
        part = pl.ds(chunk * CHUNK, CHUNK)
        return pltpu.make_async_copy(adj_ref.at[part], tiles_ref.at[part], done.at[chunk])

    for chunk in range(chunks):
        load(chunk).start()
    gather()
    acc_ref[...] = jnp.zeros_like(acc_ref)

    def product(slot):
        one, two = source(slot), source(slot + 1)
        zero = jnp.zeros_like(one)
        left = jnp.concatenate(
            [jnp.concatenate([one, zero], axis=1), jnp.concatenate([zero, two], axis=1)], axis=0
        )
        if dims is NN:
            right = tiles_ref[pl.ds(slot, 2)].reshape(2 * extent, extent)
        else:
            right = jnp.concatenate([tiles_ref[slot], tiles_ref[slot + 1]], axis=1)
        both = dot(left, right, dims)
        return both[: one.shape[0]], both[one.shape[0] :]

    @pl.loop(0, chunks)
    def _(chunk):
        load(chunk).wait()
        first = chunk * CHUNK

        @pl.when(first < count)
        def _():
            terms = [term for u in range(0, CHUNK, 2) for term in product(first + u)]
            for u, term in enumerate(terms):
                target = target_of(first + u)
                acc_ref[target] += jnp.where(first + u < count, term, 0.0)


def slots_of(table, slots):
    return lambda s: table[HEAD + s], lambda s: table[HEAD + slots + s]


def forward_kernel(
    table, adj_ref, same_ref, far_ref, keep_ref, send_ref, feat_ref, acc_ref, *tiles
):
    core, side, count = table[0], table[1], table[2]
    slots, extent, _ = adj_ref.shape
    blocks = same_ref.shape[2] // extent
    row_of, col_of = slots_of(table, slots)

    def source(slot):
        col = col_of(slot)
        nodes = pl.ds(pl.multiple_of((col % blocks) * extent, extent), extent)
        return feat_ref[col // blocks, :, nodes]

    def gather():
        for ring in range(same_ref.shape[0]):
            feat_ref[ring * SIDES + side] = same_ref[ring]
            feat_ref[ring * SIDES + 1 - side] = far_ref[ring]

    accumulate_tiles(count, gather, source, adj_ref, *tiles, acc_ref, row_of, NT)
    near, feats = keep_ref.shape[:2]
    for pair in range(near):
        keep_ref[pair] = acc_ref[pl.ds((pair * CORES + core) * feats, feats)]
        send_ref[pair] = acc_ref[pl.ds((pair * CORES + 1 - core) * feats, feats)]


def spread_kernel(value_ref, out_ref):
    for copy in range(out_ref.shape[0]):
        out_ref[copy] = value_ref[...]


def combine_kernel(near, keep_ref, received_ref, weight_ref, out_ref):
    owners, width, extent = keep_ref.shape
    halves = weight_ref.shape[1] // extent
    out_ref[:, :width] = (keep_ref[...] + received_ref[...]).astype(out_ref.dtype)
    top = pl.multiple_of((near[0] // halves) * PIECE, PIECE)
    left = pl.multiple_of((near[0] % halves) * extent, extent)
    piece = weight_ref[pl.ds(top, PIECE), pl.ds(left, extent)]
    for owner in range(owners):
        out_ref[owner, width:] = piece


def dense_kernel(terms_ref, grad_ref, out_ref, act_ref, weight_ref):
    near, feats, height, extent = terms_ref.shape
    width = height - PIECE
    full = feats * width
    halves = full // extent
    for pair in range(near):
        for feat in range(feats):
            top = feat * width + (pair // halves) * PIECE
            left = (pair % halves) * extent
            weight_ref[top : top + PIECE, left : left + extent] = terms_ref[pair, feat, width:]
    weight = weight_ref[...]
    summed = jnp.sum(terms_ref[:, :, :width].astype(jnp.float32), axis=0).reshape(full, extent)
    high = summed.astype(jnp.bfloat16)
    low = (summed - high.astype(jnp.float32)).astype(jnp.bfloat16)
    pre_act = dot(high, weight, TN) + dot(low, weight, TN)
    gate = jax.nn.sigmoid(pre_act)
    act_ref[...] = (pre_act * gate).astype(act_ref.dtype)
    derivative = gate * (1.0 + pre_act * (1.0 - gate))
    grad_pre = (grad_ref[...].astype(jnp.float32) * derivative).astype(jnp.bfloat16)
    projected = dot(weight, grad_pre, NT).astype(out_ref.dtype)
    weight_term = (dot(high, grad_pre, NN) + dot(low, grad_pre, NN)).astype(out_ref.dtype)
    for pair in range(near):
        for feat in range(feats):
            top = feat * width + (pair // halves) * PIECE
            left = (pair % halves) * extent
            out_ref[pair * feats + feat, :width] = projected[feat * width : (feat + 1) * width]
            out_ref[pair * feats + feat, width:] = weight_term[
                top : top + PIECE, left : left + extent
            ]


def backward_kernel(
    table, adj_ref, mine_ref, other_ref, out_ref, proj_ref, acc_ref, *tiles
):
    core, side, count = table[0], table[1], table[2]
    row_of, col_of = slots_of(table, adj_ref.shape[0])
    rings = out_ref.shape[0]
    width = acc_ref.shape[1]
    blocks = acc_ref.shape[0] // (rings * SIDES)
    feats = proj_ref.shape[2]

    def gather():
        for pair in range(proj_ref.shape[0]):
            part = slice(pair * feats, (pair + 1) * feats)
            proj_ref[pair, core] = mine_ref[part, :width]
            proj_ref[pair, 1 - core] = other_ref[part, :width]

    def source(slot):
        row = row_of(slot)
        return proj_ref[row // (CORES * feats), (row // feats) % CORES, row % feats]

    accumulate_tiles(count, gather, source, adj_ref, *tiles, acc_ref, col_of, NN)
    weight_term = jnp.sum(mine_ref[:, width:].astype(jnp.float32), axis=0) + jnp.sum(
        other_ref[:, width:].astype(jnp.float32), axis=0
    )
    for ring in range(rings):
        for part, out_side in enumerate((1 - side, side)):
            start = (ring * SIDES + out_side) * blocks
            for block in range(blocks):
                top = (part * blocks + block) * width
                out_ref[ring, top : top + width] = acc_ref[start + block].astype(out_ref.dtype)
        out_ref[ring, SIDES * blocks * width :] = weight_term.astype(out_ref.dtype)


def reduce_kernel(pieces_ref, far_ref, same_ref, weight_ref):
    rows = far_ref.shape[0]
    far_ref[...] = jnp.sum(pieces_ref[:, :rows].astype(jnp.float32), axis=0).astype(far_ref.dtype)
    same_ref[...] = jnp.sum(pieces_ref[:, rows : 2 * rows].astype(jnp.float32), axis=0)
    weight_term = jnp.sum(pieces_ref[:, 2 * rows :].astype(jnp.float32), axis=0)
    for copy in range(weight_ref.shape[0]):
        weight_ref[copy] = weight_term


def final_kernel(scale, same_ref, swapped_ref, terms_ref, grad_ref, weight_ref):
    width, nodes = grad_ref.shape
    extent = same_ref.shape[1]
    for block in range(nodes // extent):
        part = slice(block * width, (block + 1) * width)
        grad_ref[:, block * extent : (block + 1) * extent] = same_ref[part] + swapped_ref[
            part
        ].astype(jnp.float32)
    halves = weight_ref.shape[1] // extent
    near = terms_ref.shape[0] // SIDES
    for pair in range(near):
        top, left = (pair // halves) * PIECE, (pair % halves) * extent
        weight_ref[top : top + PIECE, left : left + extent] = (
            terms_ref[pair] + terms_ref[near + pair]
        ) * scale


SMEM_SPEC = pl.BlockSpec(memory_space=pltpu.SMEM)
VMEM_SPEC = pl.BlockSpec(memory_space=pltpu.VMEM)


def in_vmem(array):
    return pltpu.with_memory_space_constraint(array, pltpu.VMEM)


def call(kernel, scalars, arrays, out_shapes, scratch=()):
    return pl.pallas_call(
        kernel,
        out_shape=out_shapes,
        in_specs=[SMEM_SPEC] * len(scalars) + [VMEM_SPEC] * len(arrays),
        out_specs=jax.tree.map(lambda _: VMEM_SPEC, out_shapes),
        scratch_shapes=scratch,
        compiler_params=pltpu.CompilerParams(vmem_limit_bytes=VMEM_LIMIT),
    )(*scalars, *(in_vmem(array) for array in arrays))


def tile_call(kernel, scalars, adjacency, arrays, out_shapes, scratch):
    return pl.pallas_call(
        kernel,
        out_shape=out_shapes,
        in_specs=[SMEM_SPEC] * len(scalars)
        + [pl.BlockSpec(memory_space=pltpu.HBM)]
        + [VMEM_SPEC] * len(arrays),
        out_specs=jax.tree.map(lambda _: VMEM_SPEC, out_shapes),
        scratch_shapes=[
            *scratch,
            pltpu.VMEM(adjacency.shape, adjacency.dtype),
            pltpu.SemaphoreType.DMA((adjacency.shape[0] // CHUNK,)),
        ],
        compiler_params=pltpu.CompilerParams(vmem_limit_bytes=VMEM_LIMIT),
    )(
        *scalars,
        pltpu.with_memory_space_constraint(adjacency, pltpu.HBM),
        *(in_vmem(array) for array in arrays),
    )


def local(features, weight, grad_out, adjacency, tile_rows, tile_cols, tile_count):
    nodes, width = features.shape
    extent = adjacency.shape[1]
    rings, near, feats = (lax.axis_size(name) for name in ("ring", "near", "feat"))
    full = feats * width
    blocks = nodes // extent
    owners = near * feats
    swap = [(0, 1), (1, 0)]
    core, side, near_index = (
        lax.axis_index(name).astype(jnp.int32) for name in ("core", "side", "near")
    )
    table = jnp.concatenate([jnp.stack([core, side]), tile_count, tile_rows, tile_cols])
    bf16, f32 = jnp.bfloat16, jnp.float32

    def spread(value):
        copies = call(spread_kernel, (), (value,), pltpu.VMEM((rings, width, nodes), bf16))
        return lax.all_to_all(copies, "ring", 0, 0, tiled=False)

    own = features.T
    partner = lax.ppermute(own, "side", swap)
    same = spread(own)
    same, partner, table = lax.optimization_barrier((same, partner, table))
    far = spread(partner)

    half = jax.ShapeDtypeStruct((near, feats, width, extent), f32)
    keep, send = tile_call(
        forward_kernel,
        (table,),
        adjacency,
        (same, far),
        (half, half),
        [
            pltpu.VMEM((rings * SIDES, width, nodes), bf16),
            pltpu.VMEM((CORES * owners, width, extent), f32),
        ],
    )
    received = lax.ppermute(send, "core", swap)
    flat = (owners, width, extent)
    terms = call(
        combine_kernel,
        (near_index.reshape(1),),
        (keep.reshape(flat), received.reshape(flat), weight),
        pltpu.VMEM((owners, width + PIECE, extent), bf16),
    )
    terms = lax.all_to_all(terms, ("near", "feat"), 0, 0, tiled=False)
    outgoing, activated = call(
        dense_kernel,
        (),
        (terms.reshape(near, feats, width + PIECE, extent), grad_out),
        (
            pltpu.VMEM((owners, width + PIECE, extent), bf16),
            jax.ShapeDtypeStruct((extent, full), bf16),
        ),
        [pltpu.VMEM((full, full), bf16)],
    )

    mine = lax.all_to_all(outgoing, ("near", "feat"), 0, 0, tiled=False)
    other = lax.ppermute(mine, "core", swap)
    pieces = tile_call(
        backward_kernel,
        (table,),
        adjacency,
        (mine, other),
        pltpu.VMEM((rings, SIDES * blocks * width + PIECE, extent), bf16),
        [
            pltpu.VMEM((near, CORES, feats, width, extent), bf16),
            pltpu.VMEM((rings * SIDES * blocks, width, extent), f32),
        ],
    )
    pieces = lax.all_to_all(pieces, "ring", 0, 0, tiled=False)
    block_sum = (blocks * width, extent)
    other_side, this_side, weight_piece = call(
        reduce_kernel,
        (),
        (pieces,),
        (
            pltpu.VMEM(block_sum, bf16),
            jax.ShapeDtypeStruct(block_sum, f32),
            pltpu.VMEM((SIDES * near, PIECE, extent), f32),
        ),
    )
    swapped = lax.ppermute(other_side, "side", swap)
    weight_terms = lax.all_to_all(weight_piece, ("side", "near"), 0, 0, tiled=False)
    scale = 1.0 / math.sqrt(nodes * rings * SIDES * near * CORES)
    feature_grad, weight_grad = call(
        lambda *refs: final_kernel(scale, *refs),
        (),
        (this_side, swapped, weight_terms),
        (
            jax.ShapeDtypeStruct((width, nodes), f32),
            jax.ShapeDtypeStruct((width, full), f32),
        ),
    )
    return (activated, weight_grad, feature_grad.T)


def solution(mesh):
    rows, cols, feats = (mesh.shape[name] for name in ("row", "col", "feat"))
    fine = jax.sharding.Mesh(
        mesh.devices.reshape(rows // SIDES, SIDES, cols // CORES, CORES, feats),
        ("ring", "side", "near", "core", "feat"),
    )
    pair = P(("ring", "side", "near", "core"))
    owner = P(("ring", "side", "near", "core", "feat"), None)
    by_column = P(("near", "core", "ring", "side"), "feat")
    return jax.shard_map(
        local,
        mesh=fine,
        in_specs=(by_column, P("feat", None), owner, pair, pair, pair, pair),
        out_specs=(owner, P("feat", None), by_column),
        check_vma=False,
    )
```
